512 devices in a mesh: gx: 16 (over y, z_lo), gy: 32 (over x, z_hi, core).
Axes of the slice: x: 4, y: 8, z: 8 (z_hi: 4, z_lo: 2; z = z_hi * 2 + z_lo), core: 2. Of those that a mesh axis runs over, the one named last changes fastest.
Arguments:
- features: float32 [32, 64, 128, 512], P('gx', 'gy'), may hold values from -6 to 6
- tile_filter: float32 [32, 64, 9, 128, 128], P('gx', 'gy'), may hold values from -0.17677669 to 0.17677669
- positions: float32 [3, 32, 64, 128], P(None, 'gx', 'gy'), may hold values from 0 to 1, as said below
- wave_vectors: int32 [3, 1024], replicated, may hold values from -8 to 8, as said below
- msg_weight: float32 [512, 512], replicated, may hold values from -0.25 to 0.25
- out_gain: float32 [512], replicated, may hold values from 0.1 to 1.9
Outputs:
- updated: float32 [32, 64, 128, 512], P('gx', 'gy')
The draws below stay inside these ranges and needn't reach their ends.
Inputs may be any that keep to these rules, and one draw needn't show every extreme that they name: positions[:, a, b, t] = ((a + u) / 32, (b + v) / 64, w) with u, v, w in [0, 1): each atom lies in its tile's slab. `wave_vectors`: the 1024 vectors are distinct and nonzero, and hold at most one of each pair k, -k: the first nonzero component of each is positive.
All inputs are finite; a program needn't handle non-finite values.
Results may differ from the reference program's by a relative error of at most 0.0003.
Values sent between devices are 32-bit elements; how exact they have to be, the bound alone decides.
No kernel may reach another device: no remote copies, remote signals or barrier semaphores. Data moves between devices by JAX's collectives and lax.ppermute only.
A program may use at most 128 MiB of HBM per device.

```python
import math
import jax
import jax.numpy as jnp
from jax import lax

F = 512
K = 1024
TILE = 128
NBX = 32
NBY = 64
ATOMS = 262144


def draw_positions(key, part):
    key = jax.random.fold_in(key, 7)
    offsets = jax.random.uniform(key, (3, NBX, NBY, TILE), jnp.float32)
    index_x = jnp.arange(NBX, dtype=jnp.float32)[:, None, None]
    index_y = jnp.arange(NBY, dtype=jnp.float32)[None, :, None]
    first = (index_x + offsets[0]) / NBX
    second = (index_y + offsets[1]) / NBY
    return jnp.stack([first, second, offsets[2]], axis=0).astype(jnp.float32)


def draw_wave_vectors(key, part):
    key = jax.random.fold_in(key, 11)
    first_key, order_key = jax.random.split(key)
    half_count = 2456
    corner = 2167 + jax.random.randint(first_key, (), 0, 17)
    order = jax.random.permutation(order_key, half_count)
    ranking = jnp.where(order == corner, -1, jnp.arange(half_count, dtype=jnp.int32))
    order = order[jnp.argsort(ranking, stable=True)]
    picked = order[:K] + 2457
    comp_a = picked // 289 - 8
    comp_b = picked // 17 % 17 - 8
    comp_c = picked % 17 - 8
    return jnp.stack([comp_a, comp_b, comp_c], axis=0).astype(jnp.int32)


def shard_levels(rng, dims, cuts, least, top_value):
    def one(dim, blocks):
        heights = jax.random.uniform(jax.random.fold_in(jax.random.fold_in(rng, 6), dim), (blocks,), jnp.float32, least / len(cuts), top_value / len(cuts))
        return jnp.repeat(jnp.exp(heights), dims[dim] // blocks).reshape((-1,) + (1,) * (len(dims) - dim - 1))

    loudness = one(*cuts[0])
    for cut in cuts[1:]:
        loudness = loudness * one(*cut)
    return loudness


def normal_values(rng, dims, deviation, bound, cuts=(), held_as=jnp.bfloat16):
    values = deviation * jax.random.normal(rng, dims, jnp.float32)
    if cuts:
        values = values * shard_levels(rng, dims, cuts, -0.22, 0.18)
    return jnp.clip(values, -bound, bound).astype(held_as)


def setup_inputs(seed: int = 0) -> dict:
    seeds = jax.random.split(jax.random.key(seed), 7)
    features = normal_values(seeds[0], (NBX, NBY, TILE, F), 1.0, 6.0, ((0, 16), (1, 32)), jnp.float32)
    tile_filter = normal_values(seeds[1], (NBX, NBY, 9, TILE, TILE), (1.0 / (3 * TILE ** 0.5)), 0.17677669, ((0, 16), (1, 32)), jnp.float32)
    positions = draw_positions(jax.random.fold_in(seeds[6], 71), 0)
    wave_vectors = draw_wave_vectors(jax.random.fold_in(seeds[6], 71), 0)
    msg_weight = normal_values(seeds[4], (F, F), F ** -0.5, 0.25, (), jnp.float32)
    out_gain = jnp.clip(1.0 + 0.18 * jax.random.normal(seeds[5], (F,), jnp.float32), 0.1, 1.9)
    return dict(features=features, tile_filter=tile_filter, positions=positions, wave_vectors=wave_vectors, msg_weight=msg_weight, out_gain=out_gain)


HIGH = lax.Precision.HIGHEST

def phases(fractions, vectors):
    kf = vectors.astype(jnp.float32)
    angle = 2.0 * math.pi * (fractions[0][:, None] * kf[0][None, :] + fractions[1][:, None] * kf[1][None, :] + fractions[2][:, None] * kf[2][None, :])
    return (jnp.cos(angle), jnp.sin(angle))

def damping(vectors):
    kf = vectors.astype(jnp.float32)
    return jnp.exp(-lax.optimization_barrier(jnp.sum(kf * kf, axis=0)) / 64.0)

def reference(features, tile_filter, positions, wave_vectors, msg_weight, out_gain):
    projected = jnp.einsum('abtf,fg->abtg', features, msg_weight, precision=HIGH)
    message = jnp.zeros_like(features)
    for shift_x in (-1, 0, 1):
        for shift_y in (-1, 0, 1):
            rolled = jnp.roll(projected, (-shift_x, -shift_y), (0, 1))
            taps = tile_filter[:, :, (shift_x + 1) * 3 + shift_y + 1]
            message = message + jnp.einsum('abij,abjf->abif', taps, rolled, precision=HIGH)
    slab_pos = jnp.moveaxis(positions, 1, 0)

    def accumulate(carry, inputs):
        slab_fr, slab_feat = inputs
        cosine, sine_part = phases(slab_fr.reshape(3, -1), wave_vectors)
        flat = slab_feat.reshape(-1, F)
        term = jnp.concatenate([jnp.dot(cosine.T, flat, precision=HIGH), jnp.dot(sine_part.T, flat, precision=HIGH)], axis=1)
        return (carry + term, None)
    structure, unused = lax.scan(accumulate, jnp.zeros((K, 2 * F), jnp.float32), (slab_pos, features))
    coefficients = structure * (damping(wave_vectors) / math.sqrt(ATOMS))[:, None]

    def inverse(slab_fr):
        cosine, sine_part = phases(slab_fr.reshape(3, -1), wave_vectors)
        value = jnp.dot(cosine, coefficients[:, :F], precision=HIGH) + jnp.dot(sine_part, coefficients[:, F:], precision=HIGH)
        return (value / math.sqrt(K)).reshape(NBY, TILE, F)
    ewald = lax.map(inverse, slab_pos)
    total = message + ewald
    scale = jnp.sqrt(lax.optimization_barrier(jnp.mean(total * total, axis=-1, keepdims=True)) + 1e-06)
    return features + out_gain * (total / scale)
```

```python
import functools
import math

import jax
import jax.numpy as jnp
from jax import lax
from jax.experimental import pallas as pl
from jax.experimental.pallas import tpu as pltpu
from jax.sharding import Mesh
from jax.sharding import PartitionSpec as P

HIGH = lax.Precision.HIGHEST
F32, BF16 = jnp.float32, jnp.bfloat16
NN = (((1,), (0,)), ((), ()))
NT = (((1,), (1,)), ((), ()))
SLAB_X, SLAB_Y = ("y", "zl"), ("x", "zh", "c")
VMEM_LIMIT = 56 * 1024 * 1024


def halves(value):
    top = value.astype(BF16)
    return top, (value - top.astype(F32)).astype(BF16)


def dot(a, b, dims=NN):
    return lax.dot_general(a, b, dims, preferred_element_type=F32)


SIN_TERMS = tuple((-1) ** n * math.pi ** (2 * n + 1) / math.factorial(2 * n + 1) for n in range(6))
COS_TERMS = tuple((-1) ** n * math.pi ** (2 * n) / math.factorial(2 * n) for n in range(7))


def horner(terms, square):
    value = jnp.full_like(square, terms[-1])
    for term in terms[-2::-1]:
        value = value * square + term
    return value


def turn(fraction):
    rest = fraction - jnp.round(fraction)
    square = rest * rest
    sine = rest * horner(SIN_TERMS, square)
    cosine = horner(COS_TERMS, square)
    return 1.0 - 2.0 * (sine * sine), 2.0 * (sine * cosine)


def forward_kernel(scale, rows, place, vec, feat_a, feat_b, out, top, low, feat_split):
    atoms = place.shape[0]
    chans = feat_a.shape[1]

    @pl.when(pl.program_id(0) == 0)
    def _():
        for part, ref in enumerate((feat_a, feat_b)):
            count = ref.shape[0]
            hi, lo = halves(ref[...].T)
            feat_split[:chans, part * count : (part + 1) * count] = hi
            feat_split[chans:, part * count : (part + 1) * count] = lo

    vectors = vec[...]
    kx, ky, kz = vectors[0:1], vectors[1:2], vectors[2:3]

    @pl.loop(0, atoms // rows)
    def _(step):
        here = pl.ds(pl.multiple_of(step * rows, rows), rows)
        spot = place[here, :]
        cosine, sine = turn(spot[:, 0:1] * kx + spot[:, 1:2] * ky + spot[:, 2:3] * kz)
        for kind, value in enumerate((cosine, sine)):
            hi, lo = halves(value)
            top[kind, here, :] = hi
            low[kind, here, :] = lo

    damp = scale * jnp.exp(-(kx * kx + ky * ky + kz * kz) / 64.0)
    for kind in range(2):
        both = dot(feat_split[...], top[kind])
        total = both[:chans] + both[chans:] + dot(feat_split[:chans, :], low[kind])
        total = total * damp
        for tile in range(out.shape[1]):
            out[kind, tile] = total[:, tile * 128 : (tile + 1) * 128]


def forward(place, vec, feat_a, feat_b, scale):
    atoms, count, chans = place.shape[0], vec.shape[1], feat_a.shape[1]
    block = 256
    trig = jax.ShapeDtypeStruct((2, atoms, count), BF16)
    trig_spec = pl.BlockSpec((2, atoms, block), lambda j: (0, 0, j))
    whole = lambda a: pl.BlockSpec(a.shape, lambda j: (0, 0))
    return pl.pallas_call(
        functools.partial(forward_kernel, scale, 32),
        grid=(count // block,),
        in_specs=[whole(place), pl.BlockSpec((3, block), lambda j: (0, j)), whole(feat_a), whole(feat_b)],
        out_specs=[pl.BlockSpec((2, block // 128, chans, 128), lambda j: (0, j, 0, 0)), trig_spec, trig_spec],
        out_shape=[jax.ShapeDtypeStruct((2, count // 128, chans, 128), F32), trig, trig],
        scratch_shapes=[pltpu.VMEM((2 * chans, atoms), BF16)],
        compiler_params=pltpu.CompilerParams(vmem_limit_bytes=VMEM_LIMIT),
        cost_estimate=pl.CostEstimate(
            flops=12 * atoms * count * chans, bytes_accessed=24 * 2**20, transcendentals=0
        ),
    )(place, vec, feat_a, feat_b)


def inverse_kernel(top, low, coef, out, coef_top, coef_low):
    tiles = coef.shape[1]

    @pl.when(pl.program_id(0) == 0)
    def _():
        for kind in range(2):
            for tile in range(tiles):
                hi, lo = halves(coef[kind, tile])
                coef_top[kind, :, tile * 128 : (tile + 1) * 128] = hi
                coef_low[kind, :, tile * 128 : (tile + 1) * 128] = lo

    total = None
    for kind in range(2):
        for a, b in ((top, coef_top), (top, coef_low), (low, coef_top)):
            term = dot(a[kind], b[kind], NT)
            total = term if total is None else total + term
    out[...] = total


def inverse(top, low, coef):
    kinds, atoms, count = top.shape
    chans = coef.shape[2]
    block = 256
    trig_spec = pl.BlockSpec((kinds, block, count), lambda i: (0, i, 0))
    return pl.pallas_call(
        inverse_kernel,
        grid=(atoms // block,),
        in_specs=[trig_spec, trig_spec, pl.BlockSpec(coef.shape, lambda i: (0, 0, 0, 0))],
        out_specs=pl.BlockSpec((block, chans), lambda i: (i, 0)),
        out_shape=jax.ShapeDtypeStruct((atoms, chans), F32),
        scratch_shapes=[pltpu.VMEM((kinds, chans, count), BF16)] * 2,
        compiler_params=pltpu.CompilerParams(vmem_limit_bytes=VMEM_LIMIT),
        cost_estimate=pl.CostEstimate(
            flops=12 * atoms * count * chans, bytes_accessed=12 * 2**20, transcendentals=0
        ),
    )(top, low, coef)


def message_kernel(taps, own, up, down, left, right, out, block_top, block_low):
    a, b = pl.program_id(0), pl.program_id(1)

    @pl.when((a == 0) & (b == 0))
    def _():
        def put(row, column, value):
            hi, lo = halves(value)
            block_top[row, column] = hi
            block_low[row, column] = lo

        for i in range(2):
            put(0, 1 + i, up[0, i])
            put(3, 1 + i, down[0, i])
            for j in range(2):
                put(1 + i, 1 + j, own[i, j])
        for i in range(4):
            put(i, 0, left[i, 0])
            put(i, 3, right[i, 0])

    total = None
    for dx in range(3):
        for dy in range(3):
            hi, lo = halves(taps[0, 0, 3 * dx + dy])
            there_top, there_low = block_top[a + dx, b + dy], block_low[a + dx, b + dy]
            for left_part, right_part in ((hi, there_top), (hi, there_low), (lo, there_top)):
                term = dot(left_part, right_part)
                total = term if total is None else total + term
    out[0, 0] = total


def neighbour_sum(taps, own, up, down, left, right):
    tiles_x, tiles_y, rows, chans = own.shape
    whole = lambda a: pl.BlockSpec(a.shape, lambda i, j: (0, 0, 0, 0))
    return pl.pallas_call(
        message_kernel,
        grid=(tiles_x, tiles_y),
        in_specs=[pl.BlockSpec((1, 1) + taps.shape[2:], lambda i, j: (i, j, 0, 0, 0))]
        + [whole(a) for a in (own, up, down, left, right)],
        out_specs=pl.BlockSpec((1, 1, rows, chans), lambda i, j: (i, j, 0, 0)),
        out_shape=jax.ShapeDtypeStruct(own.shape, F32),
        scratch_shapes=[pltpu.VMEM((tiles_x + 2, tiles_y + 2, rows, chans), BF16)] * 2,
        compiler_params=pltpu.CompilerParams(vmem_limit_bytes=VMEM_LIMIT),
        cost_estimate=pl.CostEstimate(
            flops=6 * tiles_x * tiles_y * 9 * rows * rows * chans, bytes_accessed=8 * 2**20, transcendentals=0
        ),
    )(taps, own, up, down, left, right)


def update_kernel(core, message, mine, theirs, feat, gain, out):
    first = core[0] == 0
    a, b = mine[...], theirs[...]
    ewald = jnp.concatenate([jnp.where(first, a, b), jnp.where(first, b, a)], axis=1)
    total = message[...] + ewald
    scale = jnp.sqrt(jnp.mean(total * total, axis=-1, keepdims=True) + 1e-6)
    out[...] = feat[...] + gain[...] * (total / scale)


def update(core, message, ewald, theirs, feat, gain):
    atoms, chans = feat.shape
    block = 128
    rows = pl.BlockSpec((block, chans), lambda i: (i, 0))
    part = pl.BlockSpec((block, chans // 2), lambda i: (i, 0))
    return pl.pallas_call(
        update_kernel,
        grid=(atoms // block,),
        in_specs=[pl.BlockSpec(memory_space=pltpu.SMEM), rows, part, part, rows, pl.BlockSpec((1, chans), lambda i: (0, 0))],
        out_specs=rows,
        out_shape=jax.ShapeDtypeStruct((atoms, chans), F32),
    )(core, message, ewald, theirs, feat, gain)


def neighbours(cells, axis, dim):
    count = lax.axis_size(axis)
    head = lax.slice_in_dim(cells, 0, 1, axis=dim)
    tail = lax.slice_in_dim(cells, cells.shape[dim] - 1, cells.shape[dim], axis=dim)
    before = lax.ppermute(tail, axis, [(i, (i + 1) % count) for i in range(count)])
    after = lax.ppermute(head, axis, [((i + 1) % count, i) for i in range(count)])
    return before, after


def scatter(value, axes):
    count = lax.axis_size(axes)
    parts = value.reshape(count, value.shape[0] // count, value.shape[1])
    return jnp.sum(lax.all_to_all(parts, axes, 0, 0, tiled=True), axis=0)


def gather(value, axes):
    copies = jnp.broadcast_to(value[None], (lax.axis_size(axes),) + value.shape)
    return lax.all_to_all(copies, axes, 0, 0, tiled=True)


def shards(features, tile_filter, positions, wave_vectors, msg_weight, out_gain):
    tiles_x, tiles_y, tile_rows, channels = features.shape
    atoms = tiles_x * tiles_y * tile_rows
    count = wave_vectors.shape[1]
    atoms_all = atoms * lax.axis_size(SLAB_X) * lax.axis_size(SLAB_Y)
    core = lax.axis_index("c")
    swap = [(0, 1), (1, 0)]
    half = channels // 2

    flat = features.reshape(atoms, channels)
    place = positions.reshape(3, atoms).T
    keep = lax.dynamic_slice_in_dim(flat, core * half, half, 1)
    give = lax.dynamic_slice_in_dim(flat, (1 - core) * half, half, 1)
    place = jnp.concatenate([place, lax.ppermute(place, "c", swap)])
    take = lax.ppermute(give, "c", swap)
    scale = 1.0 / math.sqrt(atoms_all) / math.sqrt(count)
    partial, top, low = forward(place, wave_vectors.astype(F32), keep, take, scale)

    projected = jnp.einsum("abtf,fg->abtg", features, msg_weight, precision=HIGH)
    up, down = neighbours(projected, SLAB_X, 0)
    left, right = neighbours(jnp.concatenate([up, projected, down]), SLAB_Y, 1)
    message = neighbour_sum(tile_filter, projected, up, down, left, right)

    rows = partial.reshape(-1, 128)
    rows = scatter(rows, ("x",))
    rows = scatter(rows, ("y", "zl"))
    rows = jnp.sum(gather(rows, ("zh",)), axis=0)
    rows = gather(rows, ("y", "zl")).reshape(-1, 128)
    coef = gather(rows, ("x",)).reshape(partial.shape)

    ewald = inverse(top, low, coef)
    theirs = lax.ppermute(ewald[atoms:], "c", swap)
    out = update(
        core.reshape(1).astype(jnp.int32),
        message.reshape(atoms, channels),
        ewald[:atoms],
        theirs,
        flat,
        out_gain.reshape(1, channels),
    )
    return out.reshape(features.shape)


def solution(mesh):
    fine = Mesh(mesh.devices.reshape(8, 2, 4, 4, 2), ("y", "zl", "x", "zh", "c"))
    placed = (
        P(SLAB_X, SLAB_Y, None, None),
        P(SLAB_X, SLAB_Y, None, None, None),
        P(None, SLAB_X, SLAB_Y, None),
        P(),
        P(),
        P(),
    )
    return jax.shard_map(
        shards, mesh=fine, in_specs=placed, out_specs=P(SLAB_X, SLAB_Y, None, None), check_vma=False
    )
```

```python
import functools
import math

import jax
import jax.numpy as jnp
from jax import lax
from jax.experimental import pallas as pl
from jax.experimental.pallas import tpu as pltpu
from jax.sharding import Mesh
from jax.sharding import PartitionSpec as P

F32, BF16 = jnp.float32, jnp.bfloat16
NN = (((1,), (0,)), ((), ()))
NT = (((1,), (1,)), ((), ()))
SLAB_X, SLAB_Y = ("y", "zl"), ("x", "zh", "c")
VMEM_LIMIT = 24 * 1024 * 1024


def halves(value):
    top = value.astype(BF16)
    return top, (value - top.astype(F32)).astype(BF16)


def dot(a, b, dims=NN):
    return lax.dot_general(a, b, dims, preferred_element_type=F32)


SIN_TERMS = (4.44288292, -7.30824569, 3.60635422, -0.84611165, 0.109824516)
COS_TERMS = (1.4142135, -6.97885095, 5.73946038, -1.88355791, 0.310688028)
WHOLE = 12582912.0


def horner(terms, square):
    value = jnp.full_like(square, terms[-1])
    for term in terms[-2::-1]:
        value = value * square + term
    return value


def turn(fraction):
    rest = fraction - ((fraction + WHOLE) - WHOLE)
    square = rest * rest
    sine = rest * horner(SIN_TERMS, square)
    cosine = horner(COS_TERMS, square)
    return 1.0 - sine * sine, sine * cosine


def trig_kernel(rows, place, vec, top, low, split, angle):
    @pl.when(pl.program_id(0) == 0)
    def _():
        rest = place[...]
        for part in range(3):
            piece = rest.astype(BF16)
            split[:, 3 * part : 3 * part + 3] = piece
            rest = rest - piece.astype(F32)

    vectors = vec[...].astype(BF16)
    angle[...] = dot(split[...], jnp.concatenate([vectors] * 3))

    @pl.loop(0, place.shape[0] // rows)
    def _(step):
        here = pl.ds(pl.multiple_of(step * rows, rows), rows)
        for kind, value in enumerate(turn(angle[here, :])):
            top[kind, here, :], low[kind, here, :] = halves(value)


def trig(place, vec):
    atoms, count = place.shape[0], vec.shape[1]
    block = 256
    shape = jax.ShapeDtypeStruct((2, atoms, count), BF16)
    spec = pl.BlockSpec((2, atoms, block), lambda j: (0, 0, j))
    return pl.pallas_call(
        functools.partial(trig_kernel, 32),
        grid=(count // block,),
        in_specs=[pl.BlockSpec(place.shape, lambda j: (0, 0)), pl.BlockSpec((3, block), lambda j: (0, j))],
        out_specs=[spec, spec],
        out_shape=[shape, shape],
        scratch_shapes=[pltpu.VMEM((atoms, 9), BF16), pltpu.VMEM((atoms, block), F32)],
        compiler_params=pltpu.CompilerParams(vmem_limit_bytes=VMEM_LIMIT),
        cost_estimate=pl.CostEstimate(flops=4 * 2**30, bytes_accessed=4 * 2**20, transcendentals=0),
    )(place, vec)


def structure_kernel(scale, core, vec, feat, take, top_a, low_a, top_b, low_b, out, split):
    atoms, chans = take.shape

    @pl.when(pl.program_id(0) == 0)
    def _():
        start = pl.multiple_of(core[0] * chans, chans)
        for part, value in enumerate((feat[:, pl.ds(start, chans)], take[...])):
            split[part, :chans], split[part, chans:] = halves(value.T)

    vectors = vec[...]
    damp = scale * jnp.exp(-jnp.sum(vectors * vectors, axis=0, keepdims=True) / 64.0)
    for kind in range(2):
        both = dot(split[0], top_a[kind]) + dot(split[1], top_b[kind])
        total = both[:chans] + both[chans:]
        total = total + dot(split[0, :chans], low_a[kind]) + dot(split[1, :chans], low_b[kind])
        total = total * damp
        for tile in range(out.shape[1]):
            out[kind, tile] = total[:, tile * 128 : (tile + 1) * 128]


def structure(core, vec, feat, take, trigs, scale):
    atoms, chans = take.shape
    count = vec.shape[1]
    block = 256
    spec = pl.BlockSpec((2, atoms, block), lambda j: (0, 0, j))
    whole = lambda a: pl.BlockSpec(a.shape, lambda j: (0, 0))
    return pl.pallas_call(
        functools.partial(structure_kernel, scale),
        grid=(count // block,),
        in_specs=[pl.BlockSpec(memory_space=pltpu.SMEM), pl.BlockSpec((3, block), lambda j: (0, j)), whole(feat), whole(take)]
        + [spec] * 4,
        out_specs=pl.BlockSpec((2, block // 128, chans, 128), lambda j: (0, j, 0, 0)),
        out_shape=jax.ShapeDtypeStruct((2, count // 128, chans, 128), F32),
        scratch_shapes=[pltpu.VMEM((2, 2 * chans, atoms), BF16)],
        compiler_params=pltpu.CompilerParams(vmem_limit_bytes=VMEM_LIMIT),
        cost_estimate=pl.CostEstimate(
            flops=24 * atoms * count * chans, bytes_accessed=12 * 2**20, transcendentals=0
        ),
    )(core, vec, feat, take, *trigs)


def inverse_kernel(top, low, coef, out, coef_top, coef_low):
    tiles = coef.shape[1]

    @pl.when(pl.program_id(0) == 0)
    def _():
        for kind in range(2):
            for tile in range(tiles):
                here = slice(tile * 128, (tile + 1) * 128)
                coef_top[kind, here, :], coef_low[kind, here, :] = halves(coef[kind, tile].T)

    total = None
    for kind in range(2):
        for a, b in ((top, coef_top), (top, coef_low), (low, coef_top)):
            term = dot(a[kind], b[kind])
            total = term if total is None else total + term
    out[...] = total


def inverse(top, low, coef):
    kinds, atoms, count = top.shape
    chans = coef.shape[2]
    block = 256
    trig_spec = pl.BlockSpec((kinds, block, count), lambda i: (0, i, 0))
    return pl.pallas_call(
        inverse_kernel,
        grid=(atoms // block,),
        in_specs=[trig_spec, trig_spec, pl.BlockSpec(coef.shape, lambda i: (0, 0, 0, 0))],
        out_specs=pl.BlockSpec((block, chans), lambda i: (i, 0)),
        out_shape=jax.ShapeDtypeStruct((atoms, chans), F32),
        scratch_shapes=[pltpu.VMEM((kinds, count, chans), BF16)] * 2,
        compiler_params=pltpu.CompilerParams(vmem_limit_bytes=VMEM_LIMIT),
        cost_estimate=pl.CostEstimate(
            flops=12 * atoms * count * chans, bytes_accessed=6 * 2**20, transcendentals=0
        ),
    )(top, low, coef)


def message_kernel(taps, own, up, down, left, right, out, block_top, block_low):
    a, b = pl.program_id(0), pl.program_id(1)

    @pl.when((a == 0) & (b == 0))
    def _():
        def put(row, column, value):
            hi, lo = halves(value)
            block_top[row, column] = hi
            block_low[row, column] = lo

        for i in range(2):
            put(0, 1 + i, up[0, i])
            put(3, 1 + i, down[0, i])
            for j in range(2):
                put(1 + i, 1 + j, own[i, j])
        for i in range(4):
            put(i, 0, left[i, 0])
            put(i, 3, right[i, 0])

    total = None
    for dx in range(3):
        for dy in range(3):
            hi, lo = halves(taps[0, 0, 3 * dx + dy])
            there_top, there_low = block_top[a + dx, b + dy], block_low[a + dx, b + dy]
            for left_part, right_part in ((hi, there_top), (hi, there_low), (lo, there_top)):
                term = dot(left_part, right_part)
                total = term if total is None else total + term
    out[0, 0] = total


def neighbour_sum(taps, own, up, down, left, right):
    tiles_x, tiles_y, rows, chans = own.shape
    whole = lambda a: pl.BlockSpec(a.shape, lambda i, j: (0, 0, 0, 0))
    return pl.pallas_call(
        message_kernel,
        grid=(tiles_x, tiles_y),
        in_specs=[pl.BlockSpec((1, 1) + taps.shape[2:], lambda i, j: (i, j, 0, 0, 0))]
        + [whole(a) for a in (own, up, down, left, right)],
        out_specs=pl.BlockSpec((1, 1, rows, chans), lambda i, j: (i, j, 0, 0)),
        out_shape=jax.ShapeDtypeStruct(own.shape, F32),
        scratch_shapes=[pltpu.VMEM((tiles_x + 2, tiles_y + 2, rows, chans), BF16)] * 2,
        compiler_params=pltpu.CompilerParams(vmem_limit_bytes=VMEM_LIMIT),
        cost_estimate=pl.CostEstimate(
            flops=6 * tiles_x * tiles_y * 9 * rows * rows * chans, bytes_accessed=8 * 2**20, transcendentals=0
        ),
    )(taps, own, up, down, left, right)


def update_kernel(core, message, mine, theirs, feat, gain, out):
    first = core[0] == 0
    a, b = mine[...], theirs[...]
    ewald = jnp.concatenate([jnp.where(first, a, b), jnp.where(first, b, a)], axis=1)
    total = message[...] + ewald
    scale = jnp.sqrt(jnp.mean(total * total, axis=-1, keepdims=True) + 1e-6)
    out[...] = feat[...] + gain[...] * (total / scale)


def update(core, message, own, got, feat, gain):
    atoms, chans = feat.shape
    block = 128
    rows = pl.BlockSpec((block, chans), lambda i: (i, 0))
    part = pl.BlockSpec((block, chans // 2), lambda i: (i, 0))
    return pl.pallas_call(
        update_kernel,
        grid=(atoms // block,),
        in_specs=[pl.BlockSpec(memory_space=pltpu.SMEM), rows, part, part, rows, pl.BlockSpec((1, chans), lambda i: (0, 0))],
        out_specs=rows,
        out_shape=jax.ShapeDtypeStruct((atoms, chans), F32),
    )(core, message, own, got, feat, gain)


def neighbours(cells, axis, dim):
    count = lax.axis_size(axis)
    head = lax.slice_in_dim(cells, 0, 1, axis=dim)
    tail = lax.slice_in_dim(cells, cells.shape[dim] - 1, cells.shape[dim], axis=dim)
    before = lax.ppermute(tail, axis, [(i, (i + 1) % count) for i in range(count)])
    after = lax.ppermute(head, axis, [((i + 1) % count, i) for i in range(count)])
    return before, after


def scatter(value, axes):
    count = lax.axis_size(axes)
    parts = value.reshape(count, value.shape[0] // count, value.shape[1])
    return jnp.sum(lax.all_to_all(parts, axes, 0, 0, tiled=True), axis=0)


def gather(value, axes):
    copies = jnp.broadcast_to(value[None], (lax.axis_size(axes),) + value.shape)
    return lax.all_to_all(copies, axes, 0, 0, tiled=True)


def shards(features, tile_filter, positions, wave_vectors, msg_weight, out_gain):
    tiles_x, tiles_y, tile_rows, channels = features.shape
    atoms = tiles_x * tiles_y * tile_rows
    count = wave_vectors.shape[1]
    atoms_all = atoms * lax.axis_size(SLAB_X) * lax.axis_size(SLAB_Y)
    core = lax.axis_index("c")
    which = core.reshape(1).astype(jnp.int32)
    swap = [(0, 1), (1, 0)]
    half = channels // 2
    scale = 1.0 / math.sqrt(atoms_all) / math.sqrt(count)

    flat = features.reshape(atoms, channels)
    vec = wave_vectors.astype(F32)
    place = positions.reshape(3, atoms).T
    take = lax.ppermute(lax.dynamic_slice_in_dim(flat, (1 - core) * half, half, 1), "c", swap)
    other = lax.ppermute(place, "c", swap)
    projected = jnp.einsum("abtf,fg->abtg", features, msg_weight, precision=lax.Precision.HIGH)
    up, down = neighbours(projected, SLAB_X, 0)
    place, _ = lax.optimization_barrier((place, projected))
    mine = trig(place, vec)
    other, _ = lax.optimization_barrier((other, mine[0]))
    theirs = trig(other, vec)
    partial = structure(which, vec, flat, take, (*mine, *theirs), scale)

    rows, up, down = lax.optimization_barrier((partial.reshape(-1, 128), up, down))
    left, right = neighbours(jnp.concatenate([up, projected, down]), SLAB_Y, 1)
    rows = scatter(rows, ("x",))
    rows, left, right = lax.optimization_barrier((rows, left, right))
    message = neighbour_sum(tile_filter, projected, up, down, left, right)
    rows = scatter(rows, ("y", "zl"))
    rows, message = lax.optimization_barrier((rows, message))
    rows = jnp.sum(gather(rows, ("zh",)), axis=0)
    rows = gather(rows, ("y", "zl")).reshape(-1, 128)
    coef = gather(rows, ("x",)).reshape(partial.shape)

    given = inverse(*theirs, coef)
    got = lax.ppermute(given, "c", swap)
    coef, _ = lax.optimization_barrier((coef, given))
    own = inverse(*mine, coef)
    out = update(which, message.reshape(atoms, channels), own, got, flat, out_gain.reshape(1, channels))
    return out.reshape(features.shape)


def solution(mesh):
    fine = Mesh(mesh.devices.reshape(8, 2, 4, 4, 2), ("y", "zl", "x", "zh", "c"))
    placed = (
        P(SLAB_X, SLAB_Y, None, None),
        P(SLAB_X, SLAB_Y, None, None, None),
        P(None, SLAB_X, SLAB_Y, None),
        P(),
        P(),
        P(),
    )
    return jax.shard_map(
        shards, mesh=fine, in_specs=placed, out_specs=P(SLAB_X, SLAB_Y, None, None), check_vma=False
    )
```

```python
import functools
import math

import jax
import jax.numpy as jnp
from jax import lax
from jax.experimental import pallas as pl
from jax.experimental.pallas import tpu as pltpu
from jax.sharding import Mesh
from jax.sharding import PartitionSpec as P

F32, BF16 = jnp.float32, jnp.bfloat16
NN = (((1,), (0,)), ((), ()))
NT = (((1,), (1,)), ((), ()))
SLAB_X, SLAB_Y = ("y", "zl"), ("x", "zh", "c")
VMEM_LIMIT = 24 * 1024 * 1024


def halves(value):
    top = value.astype(BF16)
    return top, (value - top.astype(F32)).astype(BF16)


def dot(a, b, dims=NN):
    return lax.dot_general(a, b, dims, preferred_element_type=F32)


SIN_TERMS = (4.44288292, -7.30824569, 3.60635422, -0.84611165, 0.109824516)
COS_TERMS = (1.4142135, -6.97885095, 5.73946038, -1.88355791, 0.310688028)
WHOLE = 12582912.0


def horner(terms, square):
    value = jnp.full_like(square, terms[-1])
    for term in terms[-2::-1]:
        value = value * square + term
    return value


def turn(fraction):
    rest = fraction - ((fraction + WHOLE) - WHOLE)
    square = rest * rest
    sine = rest * horner(SIN_TERMS, square)
    cosine = horner(COS_TERMS, square)
    return 1.0 - sine * sine, sine * cosine


def trig_kernel(rows, place, vec, top, low, split, angle):
    @pl.when(pl.program_id(0) == 0)
    def _():
        rest = place[...]
        for part in range(3):
            piece = rest.astype(BF16)
            split[:, 3 * part : 3 * part + 3] = piece
            rest = rest - piece.astype(F32)

    vectors = vec[...].astype(BF16)
    angle[...] = dot(split[...], jnp.concatenate([vectors] * 3))

    @pl.loop(0, place.shape[0] // rows)
    def _(step):
        here = pl.ds(pl.multiple_of(step * rows, rows), rows)
        for kind, value in enumerate(turn(angle[here, :])):
            top[kind, here, :], low[kind, here, :] = halves(value)


def trig(place, vec):
    atoms, count = place.shape[0], vec.shape[1]
    block = 256
    shape = jax.ShapeDtypeStruct((2, atoms, count), BF16)
    spec = pl.BlockSpec((2, atoms, block), lambda j: (0, 0, j))
    return pl.pallas_call(
        functools.partial(trig_kernel, 32),
        grid=(count // block,),
        in_specs=[pl.BlockSpec(place.shape, lambda j: (0, 0)), pl.BlockSpec((3, block), lambda j: (0, j))],
        out_specs=[spec, spec],
        out_shape=[shape, shape],
        scratch_shapes=[pltpu.VMEM((atoms, 9), BF16), pltpu.VMEM((atoms, block), F32)],
        compiler_params=pltpu.CompilerParams(vmem_limit_bytes=VMEM_LIMIT),
        cost_estimate=pl.CostEstimate(flops=4 * 2**30, bytes_accessed=4 * 2**20, transcendentals=0),
    )(place, vec)


def structure_kernel(scale, core, vec, feat, take, top_a, low_a, top_b, low_b, out, split):
    atoms, chans = take.shape

    @pl.when(pl.program_id(0) == 0)
    def _():
        start = pl.multiple_of(core[0] * chans, chans)
        for part, value in enumerate((feat[:, pl.ds(start, chans)], take[...])):
            split[part, :chans], split[part, chans:] = halves(value.T)

    vectors = vec[...]
    damp = scale * jnp.exp(-jnp.sum(vectors * vectors, axis=0, keepdims=True) / 64.0)
    for kind in range(2):
        both = dot(split[0], top_a[kind]) + dot(split[1], top_b[kind])
        total = both[:chans] + both[chans:]
        total = total + dot(split[0, :chans], low_a[kind]) + dot(split[1, :chans], low_b[kind])
        total = total * damp
        for tile in range(out.shape[1]):
            out[kind, tile] = total[:, tile * 128 : (tile + 1) * 128]


def structure(core, vec, feat, take, trigs, scale):
    atoms, chans = take.shape
    count = vec.shape[1]
    block = 256
    spec = pl.BlockSpec((2, atoms, block), lambda j: (0, 0, j))
    whole = lambda a: pl.BlockSpec(a.shape, lambda j: (0, 0))
    return pl.pallas_call(
        functools.partial(structure_kernel, scale),
        grid=(count // block,),
        in_specs=[pl.BlockSpec(memory_space=pltpu.SMEM), pl.BlockSpec((3, block), lambda j: (0, j)), whole(feat), whole(take)]
        + [spec] * 4,
        out_specs=pl.BlockSpec((2, block // 128, chans, 128), lambda j: (0, j, 0, 0)),
        out_shape=jax.ShapeDtypeStruct((2, count // 128, chans, 128), F32),
        scratch_shapes=[pltpu.VMEM((2, 2 * chans, atoms), BF16)],
        compiler_params=pltpu.CompilerParams(vmem_limit_bytes=VMEM_LIMIT),
        cost_estimate=pl.CostEstimate(
            flops=24 * atoms * count * chans, bytes_accessed=12 * 2**20, transcendentals=0
        ),
    )(core, vec, feat, take, *trigs)


def inverse_kernel(top, low, coef, out, coef_top, coef_low):
    tiles = coef.shape[1]

    @pl.when(pl.program_id(0) == 0)
    def _():
        for kind in range(2):
            for tile in range(tiles):
                here = slice(tile * 128, (tile + 1) * 128)
                coef_top[kind, here, :], coef_low[kind, here, :] = halves(coef[kind, tile].T)

    total = None
    for kind in range(2):
        for a, b in ((top, coef_top), (top, coef_low), (low, coef_top)):
            term = dot(a[kind], b[kind])
            total = term if total is None else total + term
    out[...] = total


def inverse(top, low, coef):
    kinds, atoms, count = top.shape
    chans = coef.shape[2]
    block = 256
    trig_spec = pl.BlockSpec((kinds, block, count), lambda i: (0, i, 0))
    return pl.pallas_call(
        inverse_kernel,
        grid=(atoms // block,),
        in_specs=[trig_spec, trig_spec, pl.BlockSpec(coef.shape, lambda i: (0, 0, 0, 0))],
        out_specs=pl.BlockSpec((block, chans), lambda i: (i, 0)),
        out_shape=jax.ShapeDtypeStruct((atoms, chans), F32),
        scratch_shapes=[pltpu.VMEM((kinds, count, chans), BF16)] * 2,
        compiler_params=pltpu.CompilerParams(vmem_limit_bytes=VMEM_LIMIT),
        cost_estimate=pl.CostEstimate(
            flops=12 * atoms * count * chans, bytes_accessed=6 * 2**20, transcendentals=0
        ),
    )(top, low, coef)


def message_kernel(taps, own, up, down, left, right, out, block_top, block_low):
    a, b = pl.program_id(0), pl.program_id(1)

    @pl.when((a == 0) & (b == 0))
    def _():
        def put(row, column, value):
            hi, lo = halves(value)
            block_top[row, column] = hi
            block_low[row, column] = lo

        for i in range(2):
            put(0, 1 + i, up[0, i])
            put(3, 1 + i, down[0, i])
            for j in range(2):
                put(1 + i, 1 + j, own[i, j])
        for i in range(4):
            put(i, 0, left[i, 0])
            put(i, 3, right[i, 0])

    total = None
    for dx in range(3):
        for dy in range(3):
            hi, lo = halves(taps[0, 0, 3 * dx + dy])
            there_top, there_low = block_top[a + dx, b + dy], block_low[a + dx, b + dy]
            for left_part, right_part in ((hi, there_top), (hi, there_low), (lo, there_top)):
                term = dot(left_part, right_part)
                total = term if total is None else total + term
    out[0, 0] = total


def neighbour_sum(taps, own, up, down, left, right):
    tiles_x, tiles_y, rows, chans = own.shape
    whole = lambda a: pl.BlockSpec(a.shape, lambda i, j: (0, 0, 0, 0))
    return pl.pallas_call(
        message_kernel,
        grid=(tiles_x, tiles_y),
        in_specs=[pl.BlockSpec((1, 1) + taps.shape[2:], lambda i, j: (i, j, 0, 0, 0))]
        + [whole(a) for a in (own, up, down, left, right)],
        out_specs=pl.BlockSpec((1, 1, rows, chans), lambda i, j: (i, j, 0, 0)),
        out_shape=jax.ShapeDtypeStruct(own.shape, F32),
        scratch_shapes=[pltpu.VMEM((tiles_x + 2, tiles_y + 2, rows, chans), BF16)] * 2,
        compiler_params=pltpu.CompilerParams(vmem_limit_bytes=VMEM_LIMIT),
        cost_estimate=pl.CostEstimate(
            flops=6 * tiles_x * tiles_y * 9 * rows * rows * chans, bytes_accessed=8 * 2**20, transcendentals=0
        ),
    )(taps, own, up, down, left, right)


def update_kernel(core, message, mine, theirs, feat, gain, out):
    first = core[0] == 0
    a, b = mine[...], theirs[...]
    ewald = jnp.concatenate([jnp.where(first, a, b), jnp.where(first, b, a)], axis=1)
    total = message[...] + ewald
    scale = jnp.sqrt(jnp.mean(total * total, axis=-1, keepdims=True) + 1e-6)
    out[...] = feat[...] + gain[...] * (total / scale)


def update(core, message, own, got, feat, gain):
    atoms, chans = feat.shape
    block = 128
    rows = pl.BlockSpec((block, chans), lambda i: (i, 0))
    part = pl.BlockSpec((block, chans // 2), lambda i: (i, 0))
    return pl.pallas_call(
        update_kernel,
        grid=(atoms // block,),
        in_specs=[pl.BlockSpec(memory_space=pltpu.SMEM), rows, part, part, rows, pl.BlockSpec((1, chans), lambda i: (0, 0))],
        out_specs=rows,
        out_shape=jax.ShapeDtypeStruct((atoms, chans), F32),
        compiler_params=pltpu.CompilerParams(vmem_limit_bytes=8 * 1024 * 1024),
        cost_estimate=pl.CostEstimate(flops=10 * atoms * chans, bytes_accessed=4 * 2**20, transcendentals=0),
    )(core, message, own, got, feat, gain)


def neighbours(cells, axis, dim):
    count = lax.axis_size(axis)
    head = lax.slice_in_dim(cells, 0, 1, axis=dim)
    tail = lax.slice_in_dim(cells, cells.shape[dim] - 1, cells.shape[dim], axis=dim)
    before = lax.ppermute(tail, axis, [(i, (i + 1) % count) for i in range(count)])
    after = lax.ppermute(head, axis, [((i + 1) % count, i) for i in range(count)])
    return before, after


def scatter(value, axes):
    count = lax.axis_size(axes)
    parts = value.reshape(count, value.shape[0] // count, value.shape[1])
    return jnp.sum(lax.all_to_all(parts, axes, 0, 0, tiled=True), axis=0)


def gather(value, axes):
    copies = jnp.broadcast_to(value[None], (lax.axis_size(axes),) + value.shape)
    return lax.all_to_all(copies, axes, 0, 0, tiled=True)


def shards(features, tile_filter, positions, wave_vectors, msg_weight, out_gain):
    tiles_x, tiles_y, tile_rows, channels = features.shape
    atoms = tiles_x * tiles_y * tile_rows
    count = wave_vectors.shape[1]
    atoms_all = atoms * lax.axis_size(SLAB_X) * lax.axis_size(SLAB_Y)
    core = lax.axis_index("c")
    which = core.reshape(1).astype(jnp.int32)
    swap = [(0, 1), (1, 0)]
    half = channels // 2
    scale = 1.0 / math.sqrt(atoms_all) / math.sqrt(count)

    flat = features.reshape(atoms, channels)
    vec = wave_vectors.astype(F32)
    projected = jnp.einsum("abtf,fg->abtg", features, msg_weight, precision=lax.Precision.HIGH)
    up, down = neighbours(projected, SLAB_X, 0)
    place, give, _ = lax.optimization_barrier((positions, flat, projected))
    place = place.reshape(3, atoms).T
    other = lax.ppermute(place, "c", swap)
    take = lax.ppermute(lax.dynamic_slice_in_dim(give, (1 - core) * half, half, 1), "c", swap)
    mine = trig(place, vec)
    other, _ = lax.optimization_barrier((other, mine[0]))
    theirs = trig(other, vec)
    partial = structure(which, vec, flat, take, (*mine, *theirs), scale)

    rows, up, down = lax.optimization_barrier((partial.reshape(-1, 128), up, down))
    rows = scatter(rows, ("x", "zl"))
    rows, up, down = lax.optimization_barrier((rows, up, down))
    left, right = neighbours(jnp.concatenate([up, projected, down]), SLAB_Y, 1)
    rows = scatter(rows, ("y",))
    rows = jnp.sum(gather(rows, ("zh",)), axis=0)
    rows = gather(rows, ("y",)).reshape(-1, 128)
    rows, left, right = lax.optimization_barrier((rows, left, right))
    message = neighbour_sum(tile_filter, projected, up, down, left, right)
    coef = gather(rows, ("x", "zl")).reshape(partial.shape)
    coef, message = lax.optimization_barrier((coef, message))

    given = inverse(*theirs, coef)
    got = lax.ppermute(given, "c", swap)
    coef, _ = lax.optimization_barrier((coef, given))
    own = inverse(*mine, coef)
    out = update(which, message.reshape(atoms, channels), own, got, flat, out_gain.reshape(1, channels))
    return out.reshape(features.shape)


def solution(mesh):
    fine = Mesh(mesh.devices.reshape(8, 2, 4, 4, 2), ("y", "zl", "x", "zh", "c"))
    placed = (
        P(SLAB_X, SLAB_Y, None, None),
        P(SLAB_X, SLAB_Y, None, None, None),
        P(None, SLAB_X, SLAB_Y, None),
        P(),
        P(),
        P(),
    )
    return jax.shard_map(
        shards, mesh=fine, in_specs=placed, out_specs=P(SLAB_X, SLAB_Y, None, None), check_vma=False
    )
```

```python
import functools
import math

import jax
import jax.numpy as jnp
from jax import lax
from jax.experimental import pallas as pl
from jax.experimental.pallas import tpu as pltpu
from jax.sharding import Mesh
from jax.sharding import PartitionSpec as P

F32, BF16 = jnp.float32, jnp.bfloat16
NN = (((1,), (0,)), ((), ()))
NT = (((1,), (1,)), ((), ()))
SLAB_X, SLAB_Y = ("y", "zl"), ("x", "zh", "c")
VMEM_LIMIT = 16 * 1024 * 1024


def halves(value):
    top = value.astype(BF16)
    return top, (value - top.astype(F32)).astype(BF16)


def dot(a, b, dims=NN):
    return lax.dot_general(a, b, dims, preferred_element_type=F32)


SIN_TERMS = (4.44288292, -7.30824569, 3.60635422, -0.84611165, 0.109824516)
COS_TERMS = (1.4142135, -6.97885095, 5.73946038, -1.88355791, 0.310688028)
WHOLE = 12582912.0


def horner(terms, square):
    value = jnp.full_like(square, terms[-1])
    for term in terms[-2::-1]:
        value = value * square + term
    return value


def turn(fraction):
    rest = fraction - ((fraction + WHOLE) - WHOLE)
    square = rest * rest
    sine = rest * horner(SIN_TERMS, square)
    cosine = horner(COS_TERMS, square)
    return 1.0 - sine * sine, sine * cosine


def trig_kernel(rows, place, vec, top, low, split, angle):
    @pl.when(pl.program_id(0) == 0)
    def _():
        rest = place[...]
        for part in range(3):
            piece = rest.astype(BF16)
            split[:, 3 * part : 3 * part + 3] = piece
            rest = rest - piece.astype(F32)

    vectors = vec[...].astype(BF16)
    angle[...] = dot(split[...], jnp.concatenate([vectors] * 3))

    @pl.loop(0, place.shape[0] // rows)
    def _(step):
        here = pl.ds(pl.multiple_of(step * rows, rows), rows)
        for kind, value in enumerate(turn(angle[here, :])):
            top[kind, here, :], low[kind, here, :] = halves(value)


def trig(place, vec):
    atoms, count = place.shape[0], vec.shape[1]
    block = 256
    shape = jax.ShapeDtypeStruct((2, atoms, count), BF16)
    spec = pl.BlockSpec((2, atoms, block), lambda j: (0, 0, j))
    return pl.pallas_call(
        functools.partial(trig_kernel, 32),
        grid=(count // block,),
        in_specs=[pl.BlockSpec(place.shape, lambda j: (0, 0)), pl.BlockSpec((3, block), lambda j: (0, j))],
        out_specs=[spec, spec],
        out_shape=[shape, shape],
        scratch_shapes=[pltpu.VMEM((atoms, 9), BF16), pltpu.VMEM((atoms, block), F32)],
        compiler_params=pltpu.CompilerParams(vmem_limit_bytes=VMEM_LIMIT // 2),
        cost_estimate=pl.CostEstimate(flops=4 * 2**30, bytes_accessed=4 * 2**20, transcendentals=0),
    )(place, vec)


def structure_kernel(scale, core, vec, feat, take, top_a, low_a, top_b, low_b, out, split):
    atoms, chans = take.shape

    @pl.when(pl.program_id(0) == 0)
    def _():
        start = pl.multiple_of(core[0] * chans, chans)
        for part, value in enumerate((feat[:, pl.ds(start, chans)], take[...])):
            split[part, :chans], split[part, chans:] = halves(value.T)

    vectors = vec[...]
    damp = scale * jnp.exp(-jnp.sum(vectors * vectors, axis=0, keepdims=True) / 64.0)
    for kind in range(2):
        both = dot(split[0], top_a[kind]) + dot(split[1], top_b[kind])
        total = both[:chans] + both[chans:]
        total = total + dot(split[0, :chans], low_a[kind]) + dot(split[1, :chans], low_b[kind])
        total = total * damp
        for tile in range(out.shape[1]):
            out[kind, tile] = total[:, tile * 128 : (tile + 1) * 128]


def structure(core, vec, feat, take, trigs, scale):
    atoms, chans = take.shape
    count = vec.shape[1]
    block = 256
    spec = pl.BlockSpec((2, atoms, block), lambda j: (0, 0, j))
    whole = lambda a: pl.BlockSpec(a.shape, lambda j: (0, 0))
    return pl.pallas_call(
        functools.partial(structure_kernel, scale),
        grid=(count // block,),
        in_specs=[pl.BlockSpec(memory_space=pltpu.SMEM), pl.BlockSpec((3, block), lambda j: (0, j)), whole(feat), whole(take)]
        + [spec] * 4,
        out_specs=pl.BlockSpec((2, block // 128, chans, 128), lambda j: (0, j, 0, 0)),
        out_shape=jax.ShapeDtypeStruct((2, count // 128, chans, 128), F32),
        scratch_shapes=[pltpu.VMEM((2, 2 * chans, atoms), BF16)],
        compiler_params=pltpu.CompilerParams(vmem_limit_bytes=VMEM_LIMIT),
        cost_estimate=pl.CostEstimate(
            flops=24 * atoms * count * chans, bytes_accessed=12 * 2**20, transcendentals=0
        ),
    )(core, vec, feat, take, *trigs)


def inverse_kernel(top, low, coef, out, coef_top, coef_low):
    tiles = coef.shape[1]

    @pl.when(pl.program_id(0) == 0)
    def _():
        for kind in range(2):
            for tile in range(tiles):
                here = slice(tile * 128, (tile + 1) * 128)
                coef_top[kind, here, :], coef_low[kind, here, :] = halves(coef[kind, tile].T)

    total = None
    for kind in range(2):
        for a, b in ((top, coef_top), (top, coef_low), (low, coef_top)):
            term = dot(a[kind], b[kind])
            total = term if total is None else total + term
    out[...] = total


def inverse(top, low, coef):
    kinds, atoms, count = top.shape
    chans = coef.shape[2]
    block = 256
    trig_spec = pl.BlockSpec((kinds, block, count), lambda i: (0, i, 0))
    return pl.pallas_call(
        inverse_kernel,
        grid=(atoms // block,),
        in_specs=[trig_spec, trig_spec, pl.BlockSpec(coef.shape, lambda i: (0, 0, 0, 0))],
        out_specs=pl.BlockSpec((block, chans), lambda i: (i, 0)),
        out_shape=jax.ShapeDtypeStruct((atoms, chans), F32),
        scratch_shapes=[pltpu.VMEM((kinds, count, chans), BF16)] * 2,
        compiler_params=pltpu.CompilerParams(vmem_limit_bytes=VMEM_LIMIT),
        cost_estimate=pl.CostEstimate(
            flops=12 * atoms * count * chans, bytes_accessed=6 * 2**20, transcendentals=0
        ),
    )(top, low, coef)


def message_kernel(taps, own, up, down, left, right, out, block_top, block_low):
    a, b = pl.program_id(0), pl.program_id(1)

    @pl.when((a == 0) & (b == 0))
    def _():
        def put(row, column, value):
            hi, lo = halves(value)
            block_top[row, column] = hi
            block_low[row, column] = lo

        for i in range(2):
            put(0, 1 + i, up[0, i])
            put(3, 1 + i, down[0, i])
            for j in range(2):
                put(1 + i, 1 + j, own[i, j])
        for i in range(4):
            put(i, 0, left[i, 0])
            put(i, 3, right[i, 0])

    total = None
    for dx in range(3):
        for dy in range(3):
            hi, lo = halves(taps[0, 0, 3 * dx + dy])
            there_top, there_low = block_top[a + dx, b + dy], block_low[a + dx, b + dy]
            for left_part, right_part in ((hi, there_top), (hi, there_low), (lo, there_top)):
                term = dot(left_part, right_part)
                total = term if total is None else total + term
    out[0, 0] = total


def neighbour_sum(taps, own, up, down, left, right):
    tiles_x, tiles_y, rows, chans = own.shape
    whole = lambda a: pl.BlockSpec(a.shape, lambda i, j: (0, 0, 0, 0))
    return pl.pallas_call(
        message_kernel,
        grid=(tiles_x, tiles_y),
        in_specs=[pl.BlockSpec((1, 1) + taps.shape[2:], lambda i, j: (i, j, 0, 0, 0))]
        + [whole(a) for a in (own, up, down, left, right)],
        out_specs=pl.BlockSpec((1, 1, rows, chans), lambda i, j: (i, j, 0, 0)),
        out_shape=jax.ShapeDtypeStruct(own.shape, F32),
        scratch_shapes=[pltpu.VMEM((tiles_x + 2, tiles_y + 2, rows, chans), BF16)] * 2,
        compiler_params=pltpu.CompilerParams(vmem_limit_bytes=VMEM_LIMIT * 5 // 4),
        cost_estimate=pl.CostEstimate(
            flops=6 * tiles_x * tiles_y * 9 * rows * rows * chans, bytes_accessed=8 * 2**20, transcendentals=0
        ),
    )(taps, own, up, down, left, right)


def update_kernel(core, message, mine, theirs, feat, gain, out):
    first = core[0] == 0
    a, b = mine[...], theirs[...]
    ewald = jnp.concatenate([jnp.where(first, a, b), jnp.where(first, b, a)], axis=1)
    total = message[...] + ewald
    scale = jnp.sqrt(jnp.mean(total * total, axis=-1, keepdims=True) + 1e-6)
    out[...] = feat[...] + gain[...] * (total / scale)


def update(core, message, own, got, feat, gain):
    atoms, chans = feat.shape
    block = 128
    rows = pl.BlockSpec((block, chans), lambda i: (i, 0))
    part = pl.BlockSpec((block, chans // 2), lambda i: (i, 0))
    return pl.pallas_call(
        update_kernel,
        grid=(atoms // block,),
        in_specs=[pl.BlockSpec(memory_space=pltpu.SMEM), rows, part, part, rows, pl.BlockSpec((1, chans), lambda i: (0, 0))],
        out_specs=rows,
        out_shape=jax.ShapeDtypeStruct((atoms, chans), F32),
        compiler_params=pltpu.CompilerParams(vmem_limit_bytes=8 * 1024 * 1024),
        cost_estimate=pl.CostEstimate(flops=10 * atoms * chans, bytes_accessed=4 * 2**20, transcendentals=0),
    )(core, message, own, got, feat, gain)


def neighbours(cells, axis, dim):
    count = lax.axis_size(axis)
    head = lax.slice_in_dim(cells, 0, 1, axis=dim)
    tail = lax.slice_in_dim(cells, cells.shape[dim] - 1, cells.shape[dim], axis=dim)
    before = lax.ppermute(tail, axis, [(i, (i + 1) % count) for i in range(count)])
    after = lax.ppermute(head, axis, [((i + 1) % count, i) for i in range(count)])
    return before, after


def scatter(value, axes):
    count = lax.axis_size(axes)
    parts = value.reshape(count, value.shape[0] // count, value.shape[1])
    return jnp.sum(lax.all_to_all(parts, axes, 0, 0, tiled=True), axis=0)


def gather(value, axes):
    copies = jnp.broadcast_to(value[None], (lax.axis_size(axes),) + value.shape)
    return lax.all_to_all(copies, axes, 0, 0, tiled=True)


def shards(features, tile_filter, positions, wave_vectors, msg_weight, out_gain):
    tiles_x, tiles_y, tile_rows, channels = features.shape
    atoms = tiles_x * tiles_y * tile_rows
    count = wave_vectors.shape[1]
    atoms_all = atoms * lax.axis_size(SLAB_X) * lax.axis_size(SLAB_Y)
    core = lax.axis_index("c")
    which = core.reshape(1).astype(jnp.int32)
    swap = [(0, 1), (1, 0)]
    half = channels // 2
    scale = 1.0 / math.sqrt(atoms_all) / math.sqrt(count)

    flat = features.reshape(atoms, channels)
    vec = wave_vectors.astype(F32)
    place = positions.reshape(3, atoms).T
    other = lax.ppermute(place, "c", swap)
    take = lax.ppermute(lax.dynamic_slice_in_dim(flat, (1 - core) * half, half, 1), "c", swap)
    mine = trig(place, vec)
    other, _ = lax.optimization_barrier((other, mine[0]))
    theirs = trig(other, vec)
    partial = structure(which, vec, flat, take, (*mine, *theirs), scale)

    rows, cells = lax.optimization_barrier((partial.reshape(-1, 128), features))
    projected = jnp.einsum("abtf,fg->abtg", cells, msg_weight, precision=lax.Precision.HIGH)
    up, down = neighbours(projected, SLAB_X, 0)
    left, right = neighbours(jnp.concatenate([up, projected, down]), SLAB_Y, 1)
    rows = scatter(rows, ("x",))
    rows, up, down = lax.optimization_barrier((rows, up, down))
    rows = scatter(rows, ("y", "zl"))
    rows, left, right = lax.optimization_barrier((rows, left, right))
    message = neighbour_sum(tile_filter, projected, up, down, left, right)
    rows = jnp.sum(gather(rows, ("zh",)), axis=0)
    rows = gather(rows, ("y", "zl")).reshape(-1, 128)
    rows, message = lax.optimization_barrier((rows, message))
    coef = gather(rows, ("x",)).reshape(partial.shape)

    given = inverse(*theirs, coef)
    got = lax.ppermute(given, "c", swap)
    coef, _ = lax.optimization_barrier((coef, given))
    own = inverse(*mine, coef)
    out = update(which, message.reshape(atoms, channels), own, got, flat, out_gain.reshape(1, channels))
    return out.reshape(features.shape)


def solution(mesh):
    fine = Mesh(mesh.devices.reshape(8, 2, 4, 4, 2), ("y", "zl", "x", "zh", "c"))
    placed = (
        P(SLAB_X, SLAB_Y, None, None),
        P(SLAB_X, SLAB_Y, None, None, None),
        P(None, SLAB_X, SLAB_Y, None),
        P(),
        P(),
        P(),
    )
    return jax.shard_map(
        shards, mesh=fine, in_specs=placed, out_specs=P(SLAB_X, SLAB_Y, None, None), check_vma=False
    )
```

```python
import functools
import math

import jax
import jax.numpy as jnp
from jax import lax
from jax.experimental import pallas as pl
from jax.experimental.pallas import tpu as pltpu
from jax.sharding import Mesh
from jax.sharding import PartitionSpec as P

F32, BF16 = jnp.float32, jnp.bfloat16
NN = (((1,), (0,)), ((), ()))
NT = (((1,), (1,)), ((), ()))
SLAB_X, SLAB_Y = ("y", "zl"), ("x", "zh", "c")
VMEM_LIMIT = 16 * 1024 * 1024


def halves(value):
    top = value.astype(BF16)
    return top, (value - top.astype(F32)).astype(BF16)


def dot(a, b, dims=NN):
    return lax.dot_general(a, b, dims, preferred_element_type=F32)


SIN_TERMS = (4.44288292, -7.30824569, 3.60635422, -0.84611165, 0.109824516)
COS_TERMS = (1.4142135, -6.97885095, 5.73946038, -1.88355791, 0.310688028)
WHOLE = 12582912.0


def horner(terms, square):
    value = jnp.full_like(square, terms[-1])
    for term in terms[-2::-1]:
        value = value * square + term
    return value


def turn(fraction):
    rest = fraction - ((fraction + WHOLE) - WHOLE)
    square = rest * rest
    sine = rest * horner(SIN_TERMS, square)
    cosine = horner(COS_TERMS, square)
    return 1.0 - sine * sine, sine * cosine


def trig_kernel(rows, place, vec, top, low, split, angle):
    @pl.when(pl.program_id(0) == 0)
    def _():
        rest = place[...].T
        for part in range(3):
            piece = rest.astype(BF16)
            split[:, 3 * part : 3 * part + 3] = piece
            rest = rest - piece.astype(F32)

    vectors = vec[...].astype(F32).astype(BF16)
    angle[...] = dot(split[...], jnp.concatenate([vectors] * 3))

    @pl.loop(0, place.shape[1] // rows)
    def _(step):
        here = pl.ds(pl.multiple_of(step * rows, rows), rows)
        for kind, value in enumerate(turn(angle[here, :])):
            top[kind, here, :], low[kind, here, :] = halves(value)


def trig(place, vec):
    atoms, count = place.shape[1], vec.shape[1]
    block = count
    shape = jax.ShapeDtypeStruct((2, atoms, count), BF16)
    spec = pl.BlockSpec((2, atoms, block), lambda j: (0, 0, j))
    return pl.pallas_call(
        functools.partial(trig_kernel, 16),
        grid=(count // block,),
        in_specs=[pl.BlockSpec(place.shape, lambda j: (0, 0)), pl.BlockSpec((3, block), lambda j: (0, j))],
        out_specs=[spec, spec],
        out_shape=[shape, shape],
        scratch_shapes=[pltpu.VMEM((atoms, 9), BF16), pltpu.VMEM((atoms, block), F32)],
        compiler_params=pltpu.CompilerParams(vmem_limit_bytes=VMEM_LIMIT),
        cost_estimate=pl.CostEstimate(flops=4 * 2**30, bytes_accessed=4 * 2**20, transcendentals=0),
    )(place, vec)


def structure_kernel(scale, core, vec, feat, take, top_a, low_a, top_b, low_b, out, split):
    atoms, chans = take.shape

    @pl.when(pl.program_id(0) == 0)
    def _():
        start = pl.multiple_of(core[0] * chans, chans)
        for part, value in enumerate((feat[:, pl.ds(start, chans)], take[...])):
            split[part, :chans], split[part, chans:] = halves(value.T)

    vectors = vec[...].astype(F32)
    damp = scale * jnp.exp(-jnp.sum(vectors * vectors, axis=0, keepdims=True) / 64.0)
    for kind in range(2):
        both = dot(split[0], top_a[kind]) + dot(split[1], top_b[kind])
        total = both[:chans] + both[chans:]
        total = total + dot(split[0, :chans], low_a[kind]) + dot(split[1, :chans], low_b[kind])
        total = total * damp
        for tile in range(out.shape[1]):
            out[kind, tile] = total[:, tile * 128 : (tile + 1) * 128]


def structure(core, vec, feat, take, trigs, scale):
    atoms, chans = take.shape
    count = vec.shape[1]
    block = 256
    spec = pl.BlockSpec((2, atoms, block), lambda j: (0, 0, j))
    whole = lambda a: pl.BlockSpec(a.shape, lambda j: (0, 0))
    return pl.pallas_call(
        functools.partial(structure_kernel, scale),
        grid=(count // block,),
        in_specs=[pl.BlockSpec(memory_space=pltpu.SMEM), pl.BlockSpec((3, block), lambda j: (0, j)), whole(feat), whole(take)]
        + [spec] * 4,
        out_specs=pl.BlockSpec((2, block // 128, chans, 128), lambda j: (0, j, 0, 0)),
        out_shape=jax.ShapeDtypeStruct((2, count // 128, chans, 128), F32),
        scratch_shapes=[pltpu.VMEM((2, 2 * chans, atoms), BF16)],
        compiler_params=pltpu.CompilerParams(vmem_limit_bytes=VMEM_LIMIT),
        cost_estimate=pl.CostEstimate(
            flops=24 * atoms * count * chans, bytes_accessed=12 * 2**20, transcendentals=0
        ),
    )(core, vec, feat, take, *trigs)


def inverse_kernel(top, low, coef, out, coef_top, coef_low):
    tiles = coef.shape[1]

    @pl.when(pl.program_id(0) == 0)
    def _():
        for kind in range(2):
            for tile in range(tiles):
                here = slice(tile * 128, (tile + 1) * 128)
                coef_top[kind, here, :], coef_low[kind, here, :] = halves(coef[kind, tile].T)

    total = None
    for kind in range(2):
        for a, b in ((top, coef_top), (top, coef_low), (low, coef_top)):
            term = dot(a[kind], b[kind])
            total = term if total is None else total + term
    out[...] = total


def inverse(top, low, coef):
    kinds, atoms, count = top.shape
    chans = coef.shape[2]
    block = 256
    trig_spec = pl.BlockSpec((kinds, block, count), lambda i: (0, i, 0))
    return pl.pallas_call(
        inverse_kernel,
        grid=(atoms // block,),
        in_specs=[trig_spec, trig_spec, pl.BlockSpec(coef.shape, lambda i: (0, 0, 0, 0))],
        out_specs=pl.BlockSpec((block, chans), lambda i: (i, 0)),
        out_shape=jax.ShapeDtypeStruct((atoms, chans), F32),
        scratch_shapes=[pltpu.VMEM((kinds, count, chans), BF16)] * 2,
        compiler_params=pltpu.CompilerParams(vmem_limit_bytes=VMEM_LIMIT),
        cost_estimate=pl.CostEstimate(
            flops=12 * atoms * count * chans, bytes_accessed=6 * 2**20, transcendentals=0
        ),
    )(top, low, coef)


def message_kernel(taps, own, up, down, left, right, out, block_top, block_low):
    a, b = pl.program_id(0), pl.program_id(1)

    @pl.when((a == 0) & (b == 0))
    def _():
        def put(row, column, value):
            hi, lo = halves(value)
            block_top[row, column] = hi
            block_low[row, column] = lo

        for i in range(2):
            put(0, 1 + i, up[0, i])
            put(3, 1 + i, down[0, i])
            for j in range(2):
                put(1 + i, 1 + j, own[i, j])
        for i in range(4):
            put(i, 0, left[i, 0])
            put(i, 3, right[i, 0])

    total = None
    for dx in range(3):
        for dy in range(3):
            hi, lo = halves(taps[0, 0, 3 * dx + dy])
            there_top, there_low = block_top[a + dx, b + dy], block_low[a + dx, b + dy]
            for left_part, right_part in ((hi, there_top), (hi, there_low), (lo, there_top)):
                term = dot(left_part, right_part)
                total = term if total is None else total + term
    out[0, 0] = total


def neighbour_sum(taps, own, up, down, left, right):
    tiles_x, tiles_y, rows, chans = own.shape
    whole = lambda a: pl.BlockSpec(a.shape, lambda i, j: (0, 0, 0, 0))
    return pl.pallas_call(
        message_kernel,
        grid=(tiles_x, tiles_y),
        in_specs=[pl.BlockSpec((1, 1) + taps.shape[2:], lambda i, j: (i, j, 0, 0, 0))]
        + [whole(a) for a in (own, up, down, left, right)],
        out_specs=pl.BlockSpec((1, 1, rows, chans), lambda i, j: (i, j, 0, 0)),
        out_shape=jax.ShapeDtypeStruct(own.shape, F32),
        scratch_shapes=[pltpu.VMEM((tiles_x + 2, tiles_y + 2, rows, chans), BF16)] * 2,
        compiler_params=pltpu.CompilerParams(vmem_limit_bytes=VMEM_LIMIT * 5 // 4),
        cost_estimate=pl.CostEstimate(
            flops=6 * tiles_x * tiles_y * 9 * rows * rows * chans, bytes_accessed=8 * 2**20, transcendentals=0
        ),
    )(taps, own, up, down, left, right)


def update_kernel(core, message, mine, theirs, feat, gain, out):
    first = core[0] == 0
    a, b = mine[...], theirs[...]
    ewald = jnp.concatenate([jnp.where(first, a, b), jnp.where(first, b, a)], axis=1)
    total = message[...] + ewald
    scale = jnp.sqrt(jnp.mean(total * total, axis=-1, keepdims=True) + 1e-6)
    out[...] = feat[...] + gain[...] * (total / scale)


def update(core, message, own, got, feat, gain):
    atoms, chans = feat.shape
    block = 128
    rows = pl.BlockSpec((block, chans), lambda i: (i, 0))
    part = pl.BlockSpec((block, chans // 2), lambda i: (i, 0))
    return pl.pallas_call(
        update_kernel,
        grid=(atoms // block,),
        in_specs=[pl.BlockSpec(memory_space=pltpu.SMEM), rows, part, part, rows, pl.BlockSpec((1, chans), lambda i: (0, 0))],
        out_specs=rows,
        out_shape=jax.ShapeDtypeStruct((atoms, chans), F32),
        compiler_params=pltpu.CompilerParams(vmem_limit_bytes=8 * 1024 * 1024),
        cost_estimate=pl.CostEstimate(flops=10 * atoms * chans, bytes_accessed=4 * 2**20, transcendentals=0),
    )(core, message, own, got, feat, gain)


def neighbours(cells, axis, dim):
    count = lax.axis_size(axis)
    head = lax.slice_in_dim(cells, 0, 1, axis=dim)
    tail = lax.slice_in_dim(cells, cells.shape[dim] - 1, cells.shape[dim], axis=dim)
    before = lax.ppermute(tail, axis, [(i, (i + 1) % count) for i in range(count)])
    after = lax.ppermute(head, axis, [((i + 1) % count, i) for i in range(count)])
    return before, after


def scatter(value, axes):
    count = lax.axis_size(axes)
    parts = value.reshape(count, value.shape[0] // count, value.shape[1])
    return jnp.sum(lax.all_to_all(parts, axes, 0, 0, tiled=True), axis=0)


def gather(value, axes):
    copies = jnp.broadcast_to(value[None], (lax.axis_size(axes),) + value.shape)
    return lax.all_to_all(copies, axes, 0, 0, tiled=True)


def shards(features, tile_filter, positions, wave_vectors, msg_weight, out_gain):
    tiles_x, tiles_y, tile_rows, channels = features.shape
    atoms = tiles_x * tiles_y * tile_rows
    count = wave_vectors.shape[1]
    atoms_all = atoms * lax.axis_size(SLAB_X) * lax.axis_size(SLAB_Y)
    core = lax.axis_index("c")
    which = core.reshape(1).astype(jnp.int32)
    swap = [(0, 1), (1, 0)]
    half = channels // 2
    scale = 1.0 / math.sqrt(atoms_all) / math.sqrt(count)

    flat = features.reshape(atoms, channels)
    place = positions.reshape(3, atoms)
    other = lax.ppermute(place, "c", swap)
    take = lax.ppermute(lax.dynamic_slice_in_dim(flat, (1 - core) * half, half, 1), "c", swap)
    mine = trig(place, wave_vectors)
    other, _ = lax.optimization_barrier((other, mine[0]))
    theirs = trig(other, wave_vectors)
    partial = structure(which, wave_vectors, flat, take, (*mine, *theirs), scale)

    rows, cells = lax.optimization_barrier((partial.reshape(-1, 128), features))
    projected = jnp.einsum("abtf,fg->abtg", cells, msg_weight, precision=lax.Precision.HIGH)
    up, down = neighbours(projected, SLAB_X, 0)
    rows = scatter(rows, ("x",))
    rows, up, down = lax.optimization_barrier((rows, up, down))
    left, right = neighbours(jnp.concatenate([up, projected, down]), SLAB_Y, 1)
    rows = scatter(rows, ("y", "zl"))
    rows = jnp.sum(gather(rows, ("zh",)), axis=0)
    rows = gather(rows, ("y", "zl")).reshape(-1, 128)
    rows, left, right = lax.optimization_barrier((rows, left, right))
    message = neighbour_sum(tile_filter, projected, up, down, left, right)
    coef = gather(rows, ("x",)).reshape(partial.shape)
    coef, message = lax.optimization_barrier((coef, message))

    given = inverse(*theirs, coef)
    got = lax.ppermute(given, "c", swap)
    coef, _ = lax.optimization_barrier((coef, given))
    own = inverse(*mine, coef)
    out = update(which, message.reshape(atoms, channels), own, got, flat, out_gain.reshape(1, channels))
    return out.reshape(features.shape)


def solution(mesh):
    fine = Mesh(mesh.devices.reshape(8, 2, 4, 4, 2), ("y", "zl", "x", "zh", "c"))
    placed = (
        P(SLAB_X, SLAB_Y, None, None),
        P(SLAB_X, SLAB_Y, None, None, None),
        P(None, SLAB_X, SLAB_Y, None),
        P(),
        P(),
        P(),
    )
    return jax.shard_map(
        shards, mesh=fine, in_specs=placed, out_specs=P(SLAB_X, SLAB_Y, None, None), check_vma=False
    )
```

```python
import functools
import math

import jax
import jax.numpy as jnp
from jax import lax
from jax.experimental import pallas as pl
from jax.experimental.pallas import tpu as pltpu
from jax.sharding import Mesh
from jax.sharding import PartitionSpec as P

F32, BF16 = jnp.float32, jnp.bfloat16
NN = (((1,), (0,)), ((), ()))
NT = (((1,), (1,)), ((), ()))
SLAB_X, SLAB_Y = ("y", "zl"), ("x", "zh", "c")
VMEM_LIMIT = 16 * 1024 * 1024


def halves(value):
    top = value.astype(BF16)
    return top, (value - top.astype(F32)).astype(BF16)


def dot(a, b, dims=NN):
    return lax.dot_general(a, b, dims, preferred_element_type=F32)


SIN_TERMS = (4.44288292, -7.30824569, 3.60635422, -0.84611165, 0.109824516)
COS_TERMS = (1.4142135, -6.97885095, 5.73946038, -1.88355791, 0.310688028)
WHOLE = 12582912.0


def horner(terms, square):
    value = jnp.full_like(square, terms[-1])
    for term in terms[-2::-1]:
        value = value * square + term
    return value


def turn(fraction):
    rest = fraction - ((fraction + WHOLE) - WHOLE)
    square = rest * rest
    sine = rest * horner(SIN_TERMS, square)
    cosine = horner(COS_TERMS, square)
    return 1.0 - sine * sine, sine * cosine


def trig_kernel(rows, place, vec, top, low, split, angle):
    @pl.when(pl.program_id(0) == 0)
    def _():
        rest = place[...].T
        for part in range(3):
            piece = rest.astype(BF16)
            split[:, 3 * part : 3 * part + 3] = piece
            rest = rest - piece.astype(F32)

    vectors = vec[...].astype(F32).astype(BF16)
    angle[...] = dot(split[...], jnp.concatenate([vectors] * 3))

    @pl.loop(0, place.shape[1] // rows)
    def _(step):
        here = pl.ds(pl.multiple_of(step * rows, rows), rows)
        for kind, value in enumerate(turn(angle[here, :])):
            top[kind, here, :], low[kind, here, :] = halves(value)


def trig(place, vec):
    atoms, count = place.shape[1], vec.shape[1]
    block = count
    shape = jax.ShapeDtypeStruct((2, atoms, count), BF16)
    spec = pl.BlockSpec((2, atoms, block), lambda j: (0, 0, j))
    return pl.pallas_call(
        functools.partial(trig_kernel, 16),
        grid=(count // block,),
        in_specs=[pl.BlockSpec(place.shape, lambda j: (0, 0)), pl.BlockSpec((3, block), lambda j: (0, j))],
        out_specs=[spec, spec],
        out_shape=[shape, shape],
        scratch_shapes=[pltpu.VMEM((atoms, 9), BF16), pltpu.VMEM((atoms, block), F32)],
        compiler_params=pltpu.CompilerParams(vmem_limit_bytes=VMEM_LIMIT),
        cost_estimate=pl.CostEstimate(flops=4 * 2**30, bytes_accessed=4 * 2**20, transcendentals=0),
    )(place, vec)


def structure_kernel(scale, core, vec, feat, take, top_a, low_a, top_b, low_b, out, split):
    atoms, chans = take.shape

    @pl.when(pl.program_id(0) == 0)
    def _():
        start = pl.multiple_of(core[0] * chans, chans)
        for part, value in enumerate((feat[:, pl.ds(start, chans)], take[...])):
            split[part, :chans], split[part, chans:] = halves(value.T)

    vectors = vec[...].astype(F32)
    damp = scale * jnp.exp(-jnp.sum(vectors * vectors, axis=0, keepdims=True) / 64.0)
    for kind in range(2):
        both = dot(split[0], top_a[kind]) + dot(split[1], top_b[kind])
        total = both[:chans] + both[chans:]
        total = total + dot(split[0, :chans], low_a[kind]) + dot(split[1, :chans], low_b[kind])
        total = total * damp
        for tile in range(out.shape[1]):
            out[kind, tile] = total[:, tile * 128 : (tile + 1) * 128]


def structure(core, vec, feat, take, trigs, scale):
    atoms, chans = take.shape
    count = vec.shape[1]
    block = 256
    spec = pl.BlockSpec((2, atoms, block), lambda j: (0, 0, j))
    whole = lambda a: pl.BlockSpec(a.shape, lambda j: (0, 0))
    return pl.pallas_call(
        functools.partial(structure_kernel, scale),
        grid=(count // block,),
        in_specs=[pl.BlockSpec(memory_space=pltpu.SMEM), pl.BlockSpec((3, block), lambda j: (0, j)), whole(feat), whole(take)]
        + [spec] * 4,
        out_specs=pl.BlockSpec((2, block // 128, chans, 128), lambda j: (0, j, 0, 0)),
        out_shape=jax.ShapeDtypeStruct((2, count // 128, chans, 128), F32),
        scratch_shapes=[pltpu.VMEM((2, 2 * chans, atoms), BF16)],
        compiler_params=pltpu.CompilerParams(vmem_limit_bytes=VMEM_LIMIT),
        cost_estimate=pl.CostEstimate(
            flops=24 * atoms * count * chans, bytes_accessed=12 * 2**20, transcendentals=0
        ),
    )(core, vec, feat, take, *trigs)


def inverse_kernel(top, low, coef, out, coef_top, coef_low):
    span_x, span_z, span_y, piece, lanes = coef.shape
    tiles, chans = coef_top.shape[1] // lanes, coef_top.shape[2]
    per_tile = chans // piece
    per_x = span_z * span_y

    @pl.when(pl.program_id(0) == 0)
    def _():
        for tile in range(2 * tiles):
            parts = []
            for number in range(tile * per_tile, (tile + 1) * per_tile):
                here = number % per_x
                parts.append(coef[number // per_x, here % span_z, here // span_z])
            here = slice(tile % tiles * lanes, (tile % tiles + 1) * lanes)
            kind = tile // tiles
            coef_top[kind, here, :], coef_low[kind, here, :] = halves(jnp.concatenate(parts).T)

    total = None
    for kind in range(2):
        for a, b in ((top, coef_top), (top, coef_low), (low, coef_top)):
            term = dot(a[kind], b[kind])
            total = term if total is None else total + term
    out[...] = total


def inverse(top, low, coef, chans):
    kinds, atoms, count = top.shape
    block = 256
    trig_spec = pl.BlockSpec((kinds, block, count), lambda i: (0, i, 0))
    return pl.pallas_call(
        inverse_kernel,
        grid=(atoms // block,),
        in_specs=[trig_spec, trig_spec, pl.BlockSpec(coef.shape, lambda i: (0, 0, 0, 0, 0))],
        out_specs=pl.BlockSpec((block, chans), lambda i: (i, 0)),
        out_shape=jax.ShapeDtypeStruct((atoms, chans), F32),
        scratch_shapes=[pltpu.VMEM((kinds, count, chans), BF16)] * 2,
        compiler_params=pltpu.CompilerParams(vmem_limit_bytes=VMEM_LIMIT),
        cost_estimate=pl.CostEstimate(
            flops=12 * atoms * count * chans, bytes_accessed=6 * 2**20, transcendentals=0
        ),
    )(top, low, coef)


def message_kernel(taps, own, up, down, left, right, out, block_top, block_low):
    a, b = pl.program_id(0), pl.program_id(1)

    @pl.when((a == 0) & (b == 0))
    def _():
        def put(row, column, value):
            hi, lo = halves(value)
            block_top[row, column] = hi
            block_low[row, column] = lo

        for i in range(2):
            put(0, 1 + i, up[0, i])
            put(3, 1 + i, down[0, i])
            for j in range(2):
                put(1 + i, 1 + j, own[i, j])
        for i in range(4):
            put(i, 0, left[i, 0])
            put(i, 3, right[i, 0])

    total = None
    for dx in range(3):
        for dy in range(3):
            hi, lo = halves(taps[0, 0, 3 * dx + dy])
            there_top, there_low = block_top[a + dx, b + dy], block_low[a + dx, b + dy]
            for left_part, right_part in ((hi, there_top), (hi, there_low), (lo, there_top)):
                term = dot(left_part, right_part)
                total = term if total is None else total + term
    out[0, 0] = total


def neighbour_sum(taps, own, up, down, left, right):
    tiles_x, tiles_y, rows, chans = own.shape
    whole = lambda a: pl.BlockSpec(a.shape, lambda i, j: (0, 0, 0, 0))
    return pl.pallas_call(
        message_kernel,
        grid=(tiles_x, tiles_y),
        in_specs=[pl.BlockSpec((1, 1) + taps.shape[2:], lambda i, j: (i, j, 0, 0, 0))]
        + [whole(a) for a in (own, up, down, left, right)],
        out_specs=pl.BlockSpec((1, 1, rows, chans), lambda i, j: (i, j, 0, 0)),
        out_shape=jax.ShapeDtypeStruct(own.shape, F32),
        scratch_shapes=[pltpu.VMEM((tiles_x + 2, tiles_y + 2, rows, chans), BF16)] * 2,
        compiler_params=pltpu.CompilerParams(vmem_limit_bytes=VMEM_LIMIT * 5 // 4),
        cost_estimate=pl.CostEstimate(
            flops=6 * tiles_x * tiles_y * 9 * rows * rows * chans, bytes_accessed=8 * 2**20, transcendentals=0
        ),
    )(taps, own, up, down, left, right)


def update_kernel(core, message, mine, theirs, feat, gain, out):
    first = core[0] == 0
    a, b = mine[...], theirs[...]
    ewald = jnp.concatenate([jnp.where(first, a, b), jnp.where(first, b, a)], axis=1)
    total = message[...] + ewald
    scale = jnp.sqrt(jnp.mean(total * total, axis=-1, keepdims=True) + 1e-6)
    out[...] = feat[...] + gain[...] * (total / scale)


def update(core, message, own, got, feat, gain):
    atoms, chans = feat.shape
    block = 128
    rows = pl.BlockSpec((block, chans), lambda i: (i, 0))
    part = pl.BlockSpec((block, chans // 2), lambda i: (i, 0))
    return pl.pallas_call(
        update_kernel,
        grid=(atoms // block,),
        in_specs=[pl.BlockSpec(memory_space=pltpu.SMEM), rows, part, part, rows, pl.BlockSpec((1, chans), lambda i: (0, 0))],
        out_specs=rows,
        out_shape=jax.ShapeDtypeStruct((atoms, chans), F32),
        compiler_params=pltpu.CompilerParams(vmem_limit_bytes=8 * 1024 * 1024),
        cost_estimate=pl.CostEstimate(flops=10 * atoms * chans, bytes_accessed=4 * 2**20, transcendentals=0),
    )(core, message, own, got, feat, gain)


def neighbours(cells, axis, dim):
    count = lax.axis_size(axis)
    head = lax.slice_in_dim(cells, 0, 1, axis=dim)
    tail = lax.slice_in_dim(cells, cells.shape[dim] - 1, cells.shape[dim], axis=dim)
    before = lax.ppermute(tail, axis, [(i, (i + 1) % count) for i in range(count)])
    after = lax.ppermute(head, axis, [((i + 1) % count, i) for i in range(count)])
    return before, after


def scatter(value, axes):
    count = lax.axis_size(axes)
    parts = value.reshape(count, value.shape[0] // count, value.shape[1])
    return jnp.sum(lax.all_to_all(parts, axes, 0, 0, tiled=True), axis=0)


def gather(value, axes):
    copies = jnp.broadcast_to(value[None], (lax.axis_size(axes),) + value.shape)
    return lax.all_to_all(copies, axes, 0, 0, tiled=True)


def shards(features, tile_filter, positions, wave_vectors, msg_weight, out_gain):
    tiles_x, tiles_y, tile_rows, channels = features.shape
    atoms = tiles_x * tiles_y * tile_rows
    count = wave_vectors.shape[1]
    atoms_all = atoms * lax.axis_size(SLAB_X) * lax.axis_size(SLAB_Y)
    core = lax.axis_index("c")
    which = core.reshape(1).astype(jnp.int32)
    swap = [(0, 1), (1, 0)]
    half = channels // 2
    scale = 1.0 / math.sqrt(atoms_all) / math.sqrt(count)

    flat = features.reshape(atoms, channels)
    place = positions.reshape(3, atoms)
    other = lax.ppermute(place, "c", swap)
    take = lax.ppermute(lax.dynamic_slice_in_dim(flat, (1 - core) * half, half, 1), "c", swap)
    mine = trig(place, wave_vectors)
    other, _ = lax.optimization_barrier((other, mine[0]))
    theirs = trig(other, wave_vectors)
    partial = structure(which, wave_vectors, flat, take, (*mine, *theirs), scale)

    rows, cells = lax.optimization_barrier((partial.reshape(-1, 128), features))
    projected = jnp.einsum("abtf,fg->abtg", cells, msg_weight, precision=lax.Precision.HIGH)
    up, down = neighbours(projected, SLAB_X, 0)
    rows = scatter(rows, ("x",))
    rows, up, down = lax.optimization_barrier((rows, up, down))
    left, right = neighbours(jnp.concatenate([up, projected, down]), SLAB_Y, 1)
    rows = scatter(rows, ("y", "zl"))
    rows = jnp.sum(gather(rows, ("zh",)), axis=0)
    rows, left, right = lax.optimization_barrier((rows, left, right))
    rows = gather(rows, ("y",)).reshape(-1, 128)
    message = neighbour_sum(tile_filter, projected, up, down, left, right)
    coef = gather(rows, ("x", "zl"))
    coef = coef.reshape(lax.axis_size("x"), lax.axis_size("zl"), lax.axis_size("y"), -1, 128)
    coef, message = lax.optimization_barrier((coef, message))

    given = inverse(*theirs, coef, half)
    got = lax.ppermute(given, "c", swap)
    coef, _ = lax.optimization_barrier((coef, given))
    own = inverse(*mine, coef, half)
    out = update(which, message.reshape(atoms, channels), own, got, flat, out_gain.reshape(1, channels))
    return out.reshape(features.shape)


def solution(mesh):
    fine = Mesh(mesh.devices.reshape(8, 2, 4, 4, 2), ("y", "zl", "x", "zh", "c"))
    placed = (
        P(SLAB_X, SLAB_Y, None, None),
        P(SLAB_X, SLAB_Y, None, None, None),
        P(None, SLAB_X, SLAB_Y, None),
        P(),
        P(),
        P(),
    )
    return jax.shard_map(
        shards, mesh=fine, in_specs=placed, out_specs=P(SLAB_X, SLAB_Y, None, None), check_vma=False
    )
```

```python
import functools
import math

import jax
import jax.numpy as jnp
from jax import lax
from jax.experimental import pallas as pl
from jax.experimental.pallas import tpu as pltpu
from jax.sharding import Mesh
from jax.sharding import PartitionSpec as P

F32, BF16 = jnp.float32, jnp.bfloat16
NN = (((1,), (0,)), ((), ()))
NT = (((1,), (1,)), ((), ()))
SLAB_X, SLAB_Y = ("y", "zl"), ("x", "zh", "c")
VMEM_LIMIT = 16 * 1024 * 1024


def halves(value):
    top = value.astype(BF16)
    return top, (value - top.astype(F32)).astype(BF16)


def dot(a, b, dims=NN):
    return lax.dot_general(a, b, dims, preferred_element_type=F32)


SIN_TERMS = (4.44288292, -7.30824569, 3.60635422, -0.84611165, 0.109824516)
COS_TERMS = (1.4142135, -6.97885095, 5.73946038, -1.88355791, 0.310688028)
WHOLE = 12582912.0


def horner(terms, square):
    value = jnp.full_like(square, terms[-1])
    for term in terms[-2::-1]:
        value = value * square + term
    return value


def turn(fraction):
    rest = fraction - ((fraction + WHOLE) - WHOLE)
    square = rest * rest
    sine = rest * horner(SIN_TERMS, square)
    cosine = horner(COS_TERMS, square)
    return 1.0 - sine * sine, sine * cosine


def trig_kernel(rows, place, vec, top, low, split, angle):
    @pl.when(pl.program_id(0) == 0)
    def _():
        rest = place[...].T
        for part in range(3):
            piece = rest.astype(BF16)
            split[:, 3 * part : 3 * part + 3] = piece
            rest = rest - piece.astype(F32)

    vectors = vec[...].astype(F32).astype(BF16)
    angle[...] = dot(split[...], jnp.concatenate([vectors] * 3))

    @pl.loop(0, place.shape[1] // rows)
    def _(step):
        here = pl.ds(pl.multiple_of(step * rows, rows), rows)
        for kind, value in enumerate(turn(angle[here, :])):
            top[kind, here, :], low[kind, here, :] = halves(value)


def trig(place, vec):
    atoms, count = place.shape[1], vec.shape[1]
    block = count
    shape = jax.ShapeDtypeStruct((2, atoms, count), BF16)
    spec = pl.BlockSpec((2, atoms, block), lambda j: (0, 0, j))
    return pl.pallas_call(
        functools.partial(trig_kernel, 16),
        grid=(count // block,),
        in_specs=[pl.BlockSpec(place.shape, lambda j: (0, 0)), pl.BlockSpec((3, block), lambda j: (0, j))],
        out_specs=[spec, spec],
        out_shape=[shape, shape],
        scratch_shapes=[pltpu.VMEM((atoms, 9), BF16), pltpu.VMEM((atoms, block), F32)],
        compiler_params=pltpu.CompilerParams(vmem_limit_bytes=VMEM_LIMIT),
        cost_estimate=pl.CostEstimate(flops=4 * 2**30, bytes_accessed=4 * 2**20, transcendentals=0),
    )(place, vec)


def structure_kernel(scale, core, vec, feat, take, top_a, low_a, top_b, low_b, out, split):
    atoms, chans = take.shape

    @pl.when(pl.program_id(0) == 0)
    def _():
        start = pl.multiple_of(core[0] * chans, chans)
        for part, value in enumerate((feat[:, pl.ds(start, chans)], take[...])):
            split[part, :chans], split[part, chans:] = halves(value.T)

    vectors = vec[...].astype(F32)
    damp = scale * jnp.exp(-jnp.sum(vectors * vectors, axis=0, keepdims=True) / 64.0)
    for kind in range(2):
        both = dot(split[0], top_a[kind]) + dot(split[1], top_b[kind])
        total = both[:chans] + both[chans:]
        total = total + dot(split[0, :chans], low_a[kind]) + dot(split[1, :chans], low_b[kind])
        total = total * damp
        for tile in range(out.shape[1]):
            out[kind, tile] = total[:, tile * 128 : (tile + 1) * 128]


def structure(core, vec, feat, take, trigs, scale):
    atoms, chans = take.shape
    count = vec.shape[1]
    block = 256
    spec = pl.BlockSpec((2, atoms, block), lambda j: (0, 0, j))
    whole = lambda a: pl.BlockSpec(a.shape, lambda j: (0, 0))
    return pl.pallas_call(
        functools.partial(structure_kernel, scale),
        grid=(count // block,),
        in_specs=[pl.BlockSpec(memory_space=pltpu.SMEM), pl.BlockSpec((3, block), lambda j: (0, j)), whole(feat), whole(take)]
        + [spec] * 4,
        out_specs=pl.BlockSpec((2, block // 128, chans, 128), lambda j: (0, j, 0, 0)),
        out_shape=jax.ShapeDtypeStruct((2, count // 128, chans, 128), F32),
        scratch_shapes=[pltpu.VMEM((2, 2 * chans, atoms), BF16)],
        compiler_params=pltpu.CompilerParams(vmem_limit_bytes=VMEM_LIMIT),
        cost_estimate=pl.CostEstimate(
            flops=24 * atoms * count * chans, bytes_accessed=12 * 2**20, transcendentals=0
        ),
    )(core, vec, feat, take, *trigs)


def inverse_kernel(top, low, coef, out, coef_top, coef_low):
    span_x, span_z, span_y, piece, lanes = coef.shape
    tiles, chans = coef_top.shape[1] // lanes, coef_top.shape[2]
    per_tile = chans // piece
    per_x = span_z * span_y

    @pl.when(pl.program_id(0) == 0)
    def _():
        for tile in range(2 * tiles):
            parts = []
            for number in range(tile * per_tile, (tile + 1) * per_tile):
                here = number % per_x
                parts.append(coef[number // per_x, here % span_z, here // span_z])
            here = slice(tile % tiles * lanes, (tile % tiles + 1) * lanes)
            kind = tile // tiles
            coef_top[kind, here, :], coef_low[kind, here, :] = halves(jnp.concatenate(parts).T)

    total = None
    for kind in range(2):
        for a, b in ((top, coef_top), (top, coef_low), (low, coef_top)):
            term = dot(a[kind], b[kind])
            total = term if total is None else total + term
    out[...] = total


def inverse(top, low, coef, chans):
    kinds, atoms, count = top.shape
    block = 256
    trig_spec = pl.BlockSpec((kinds, block, count), lambda i: (0, i, 0))
    return pl.pallas_call(
        inverse_kernel,
        grid=(atoms // block,),
        in_specs=[trig_spec, trig_spec, pl.BlockSpec(coef.shape, lambda i: (0, 0, 0, 0, 0))],
        out_specs=pl.BlockSpec((block, chans), lambda i: (i, 0)),
        out_shape=jax.ShapeDtypeStruct((atoms, chans), F32),
        scratch_shapes=[pltpu.VMEM((kinds, count, chans), BF16)] * 2,
        compiler_params=pltpu.CompilerParams(vmem_limit_bytes=VMEM_LIMIT),
        cost_estimate=pl.CostEstimate(
            flops=12 * atoms * count * chans, bytes_accessed=6 * 2**20, transcendentals=0
        ),
    )(top, low, coef)


def message_kernel(taps, own, up, down, left, right, out, block_top, block_low):
    a, b = pl.program_id(0), pl.program_id(1)

    @pl.when((a == 0) & (b == 0))
    def _():
        def put(row, column, value):
            hi, lo = halves(value)
            block_top[row, column] = hi
            block_low[row, column] = lo

        for i in range(2):
            put(0, 1 + i, up[0, i])
            put(3, 1 + i, down[0, i])
            for j in range(2):
                put(1 + i, 1 + j, own[i, j])
        for i in range(4):
            put(i, 0, left[i, 0])
            put(i, 3, right[i, 0])

    total = None
    for dx in range(3):
        for dy in range(3):
            hi, lo = halves(taps[0, 0, 3 * dx + dy])
            there_top, there_low = block_top[a + dx, b + dy], block_low[a + dx, b + dy]
            for left_part, right_part in ((hi, there_top), (hi, there_low), (lo, there_top)):
                term = dot(left_part, right_part)
                total = term if total is None else total + term
    out[0, 0] = total


def neighbour_sum(taps, own, up, down, left, right):
    tiles_x, tiles_y, rows, chans = own.shape
    whole = lambda a: pl.BlockSpec(a.shape, lambda i, j: (0, 0, 0, 0))
    return pl.pallas_call(
        message_kernel,
        grid=(tiles_x, tiles_y),
        in_specs=[pl.BlockSpec((1, 1) + taps.shape[2:], lambda i, j: (i, j, 0, 0, 0))]
        + [whole(a) for a in (own, up, down, left, right)],
        out_specs=pl.BlockSpec((1, 1, rows, chans), lambda i, j: (i, j, 0, 0)),
        out_shape=jax.ShapeDtypeStruct(own.shape, F32),
        scratch_shapes=[pltpu.VMEM((tiles_x + 2, tiles_y + 2, rows, chans), BF16)] * 2,
        compiler_params=pltpu.CompilerParams(vmem_limit_bytes=VMEM_LIMIT * 5 // 4),
        cost_estimate=pl.CostEstimate(
            flops=6 * tiles_x * tiles_y * 9 * rows * rows * chans, bytes_accessed=8 * 2**20, transcendentals=0
        ),
    )(taps, own, up, down, left, right)


def update_kernel(core, message, mine, theirs, feat, gain, out):
    first = core[0] == 0
    a, b = mine[...], theirs[...]
    ewald = jnp.concatenate([jnp.where(first, a, b), jnp.where(first, b, a)], axis=1)
    total = message[...] + ewald
    scale = jnp.sqrt(jnp.mean(total * total, axis=-1, keepdims=True) + 1e-6)
    out[...] = feat[...] + gain[...] * (total / scale)


def update(core, message, own, got, feat, gain):
    atoms, chans = feat.shape
    block = 128
    rows = pl.BlockSpec((block, chans), lambda i: (i, 0))
    part = pl.BlockSpec((block, chans // 2), lambda i: (i, 0))
    return pl.pallas_call(
        update_kernel,
        grid=(atoms // block,),
        in_specs=[pl.BlockSpec(memory_space=pltpu.SMEM), rows, part, part, rows, pl.BlockSpec((1, chans), lambda i: (0, 0))],
        out_specs=rows,
        out_shape=jax.ShapeDtypeStruct((atoms, chans), F32),
        compiler_params=pltpu.CompilerParams(vmem_limit_bytes=8 * 1024 * 1024),
        cost_estimate=pl.CostEstimate(flops=10 * atoms * chans, bytes_accessed=4 * 2**20, transcendentals=0),
    )(core, message, own, got, feat, gain)


def neighbours(cells, axis, dim):
    count = lax.axis_size(axis)
    head = lax.slice_in_dim(cells, 0, 1, axis=dim)
    tail = lax.slice_in_dim(cells, cells.shape[dim] - 1, cells.shape[dim], axis=dim)
    before = lax.ppermute(tail, axis, [(i, (i + 1) % count) for i in range(count)])
    after = lax.ppermute(head, axis, [((i + 1) % count, i) for i in range(count)])
    return before, after


def scatter(value, axes):
    count = lax.axis_size(axes)
    parts = value.reshape(count, value.shape[0] // count, value.shape[1])
    return jnp.sum(lax.all_to_all(parts, axes, 0, 0, tiled=True), axis=0)


def gather(value, axes):
    copies = jnp.broadcast_to(value[None], (lax.axis_size(axes),) + value.shape)
    return lax.all_to_all(copies, axes, 0, 0, tiled=True)


def shards(features, tile_filter, positions, wave_vectors, msg_weight, out_gain):
    tiles_x, tiles_y, tile_rows, channels = features.shape
    atoms = tiles_x * tiles_y * tile_rows
    count = wave_vectors.shape[1]
    atoms_all = atoms * lax.axis_size(SLAB_X) * lax.axis_size(SLAB_Y)
    core = lax.axis_index("c")
    which = core.reshape(1).astype(jnp.int32)
    swap = [(0, 1), (1, 0)]
    half = channels // 2
    scale = 1.0 / math.sqrt(atoms_all) / math.sqrt(count)

    flat = features.reshape(atoms, channels)
    place = positions.reshape(3, atoms)
    other = lax.ppermute(place, "c", swap)
    take = lax.ppermute(lax.dynamic_slice_in_dim(flat, (1 - core) * half, half, 1), "c", swap)
    mine = trig(place, wave_vectors)
    other, _ = lax.optimization_barrier((other, mine[0]))
    theirs = trig(other, wave_vectors)
    partial = structure(which, wave_vectors, flat, take, (*mine, *theirs), scale)

    rows, cells = lax.optimization_barrier((partial.reshape(-1, 128), features))
    projected = jnp.einsum("abtf,fg->abtg", cells, msg_weight, precision=lax.Precision.HIGH)
    up, down = neighbours(projected, SLAB_X, 0)
    left, right = neighbours(jnp.concatenate([up, projected, down]), SLAB_Y, 1)
    rows = scatter(rows, ("x",))
    rows, up, down = lax.optimization_barrier((rows, up, down))
    rows = scatter(rows, ("y", "zl"))
    rows, right = lax.optimization_barrier((rows, right))
    rows = jnp.sum(gather(rows, ("zh",)), axis=0)
    rows, left = lax.optimization_barrier((rows, left))
    rows = gather(rows, ("y",)).reshape(-1, 128)
    message = neighbour_sum(tile_filter, projected, up, down, left, right)
    coef = gather(rows, ("x", "zl"))
    coef = coef.reshape(lax.axis_size("x"), lax.axis_size("zl"), lax.axis_size("y"), -1, 128)
    coef, message = lax.optimization_barrier((coef, message))

    given = inverse(*theirs, coef, half)
    got = lax.ppermute(given, "c", swap)
    coef, _ = lax.optimization_barrier((coef, given))
    own = inverse(*mine, coef, half)
    out = update(which, message.reshape(atoms, channels), own, got, flat, out_gain.reshape(1, channels))
    return out.reshape(features.shape)


def solution(mesh):
    fine = Mesh(mesh.devices.reshape(8, 2, 4, 4, 2), ("y", "zl", "x", "zh", "c"))
    placed = (
        P(SLAB_X, SLAB_Y, None, None),
        P(SLAB_X, SLAB_Y, None, None, None),
        P(None, SLAB_X, SLAB_Y, None),
        P(),
        P(),
        P(),
    )
    return jax.shard_map(
        shards, mesh=fine, in_specs=placed, out_specs=P(SLAB_X, SLAB_Y, None, None), check_vma=False
    )
```
